256 devices in a mesh: energy: 64 (over x, z_hi, y, core), elem: 4 (over z_lo).
Axes of the slice: x: 4, y: 4, z: 8 (z_hi: 2, z_lo: 4; z = z_hi * 4 + z_lo), core: 2. Of those that a mesh axis runs over, the one named last changes fastest.
Arguments:
- green_lesser: float32 [2, 8192, 8192], P(None, 'elem', 'energy'), may hold values from -5 to 5
- green_greater: float32 [2, 8192, 8192], P(None, 'elem', 'energy'), may hold values from -5 to 5
- screen: float32 [8192], P('elem'), may hold values from 0.5 to 2
- couple: float32 [8192], P('elem'), may hold values from 0.2 to 1
Outputs:
- polarization: float32 [2, 8192, 8192], P(None, 'elem', 'energy')
- self_energy: float32 [2, 8192, 8192], P(None, 'elem', 'energy')
The draws below stay inside these ranges and needn't reach their ends.
All inputs are finite; a program needn't handle non-finite values.
Results may differ from the reference program's by a relative error of at most 0.00013.
Values sent between devices are 32-bit elements; how exact they have to be, the bound alone decides.
No kernel may reach another device: no remote copies, remote signals or barrier semaphores. Data moves between devices by JAX's collectives and lax.ppermute only.
A program may use at most 128 MiB of HBM per device.

```python
import math
import jax
import jax.numpy as jnp
from jax import lax

NE = 8192
EL = 8192
N_ELEM = 4


def block_levels(key, shape, cuts, least, largest):
    loudness, own = 1.0, jax.random.fold_in(key, 6)
    for dim, blocks in cuts:
        heights = jnp.exp(jax.random.uniform(jax.random.fold_in(own, dim), (blocks,), jnp.float32, least / len(cuts), largest / len(cuts)))
        loudness = loudness * jnp.repeat(heights, shape[dim] // blocks).reshape([-1 if axis == dim else 1 for axis in range(len(shape))])
    return loudness


def centred(stream_key, shape, scale, most, pieces=(), kind=jnp.bfloat16):
    drawn = jax.random.normal(stream_key, shape, jnp.float32) * scale
    if len(pieces) > 0:
        drawn = block_levels(stream_key, shape, pieces, -0.22, 0.18) * drawn
    return jnp.clip(drawn, min=-most, max=most).astype(kind)


def setup_inputs(seed: int = 0) -> dict:
    seeds = jax.random.split(jax.random.key(seed), 5)
    green_lesser = centred(seeds[0], (2, EL, NE), 0.7, 5.0, ((1, 4), (2, 64)), jnp.float32)
    green_greater = centred(seeds[1], (2, EL, NE), 0.7, 5.0, ((1, 4), (2, 64)), jnp.float32)
    screen = jnp.clip(jnp.exp(math.log(2.0) - 1.3862944 * jax.random.uniform(seeds[2], (EL,), jnp.float32) ** block_levels(seeds[2], (EL,), ((0, 4),), -0.2, 0.2)), 0.5, 2.0)
    couple = jnp.clip(0.2 + 0.8 * jax.random.uniform(seeds[3], (EL,), jnp.float32) ** block_levels(seeds[3], (EL,), ((0, 4),), -0.2, 0.2), 0.2, 1.0)
    return dict(green_lesser=green_lesser, green_greater=green_greater, screen=screen, couple=couple)


def as_complex(block_part):
    return lax.complex(block_part[0], block_part[1])


def reference(green_lesser, green_greater, screen, couple):
    row_count = N_ELEM
    row_width = green_lesser.shape[1] // row_count
    length = green_lesser.shape[2]
    norm_factor = length ** -0.5

    def polar_row(row_index):
        lesser = as_complex(lax.dynamic_slice_in_dim(green_lesser, row_index * row_width, row_width, 1))
        greater = as_complex(lax.dynamic_slice_in_dim(green_greater, row_index * row_width, row_width, 1))
        summed = jnp.fft.ifft(jnp.fft.fft(lesser, axis=-1) * jnp.conj(jnp.fft.fft(greater, axis=-1)), axis=-1)
        return jnp.stack([-norm_factor * jnp.imag(summed), norm_factor * jnp.real(summed)]).astype(jnp.float32)

    polar_rows = lax.map(polar_row, jnp.arange(row_count, dtype=jnp.int32))
    polar_rows = jnp.moveaxis(polar_rows, 0, 1)
    polarization = polar_rows.reshape(2, row_count * row_width, length)
    padded = jnp.pad(polar_rows, ((0, 0), (1, 1), (0, 0), (0, 0)))
    beside = padded[:, :-2] + padded[:, 2:]
    screen_rows = screen.reshape(row_count, row_width)[None, :, :, None]
    couple_rows = couple.reshape(row_count, row_width)[None, :, :, None]
    screened = (screen_rows * polar_rows + couple_rows * beside).reshape(2, row_count * row_width, length)

    def sigma_row(row_index):
        lesser = as_complex(lax.dynamic_slice_in_dim(green_lesser, row_index * row_width, row_width, 1))
        weights = as_complex(lax.dynamic_slice_in_dim(screened, row_index * row_width, row_width, 1))
        summed = jnp.fft.ifft(jnp.fft.fft(lesser, axis=-1) * jnp.fft.fft(weights, axis=-1), axis=-1)
        return jnp.stack([-norm_factor * jnp.imag(summed), norm_factor * jnp.real(summed)]).astype(jnp.float32)

    sigma_rows = lax.map(sigma_row, jnp.arange(row_count, dtype=jnp.int32))
    self_energy = jnp.moveaxis(sigma_rows, 0, 1).reshape(2, row_count * row_width, length)
    return polarization, self_energy
```

```python
import functools
import math

import jax
import jax.numpy as jnp
import ml_dtypes
import numpy as np
from jax import lax
from jax.experimental import pallas as pl
from jax.experimental.pallas import tpu as pltpu
from jax.sharding import Mesh
from jax.sharding import PartitionSpec as P

SIZES = (4, 2, 4, 2, 4)
AXES = ("x", "zh", "y", "c", "zl")
RING = ("zh", "zl")
PLANE = ("x", "y", "c")
NZ, NU = 8, 32
NJ, NB = 64, 128
NE = NJ * NB
KK = 4
F32, BF16 = jnp.float32, jnp.bfloat16
HBM = pl.BlockSpec(memory_space=pl.ANY)
VMEM = pl.BlockSpec(memory_space=pltpu.VMEM)
SMEM = pl.BlockSpec(memory_space=pltpu.SMEM)
LIMIT = 40 * 1024 * 1024


def halves(table):
    high = table.astype(np.float32).astype(ml_dtypes.bfloat16)
    low = (table - high.astype(np.float64)).astype(np.float32).astype(ml_dtypes.bfloat16)
    return high, low


@functools.lru_cache(maxsize=1)
def tables():
    zh, u = np.meshgrid(np.arange(2), np.arange(NU), indexing="ij")
    j = ((u // 8) * 16 + zh * 8 + u % 8).reshape(-1)
    outer = 2 * math.pi * (j[:, None] * np.arange(NJ)[None, :] % NJ) / NJ
    inner = 2 * math.pi * (np.arange(NB)[:, None] * np.arange(NB)[None, :] % NB) / NB
    twist = 2 * math.pi * (np.arange(NJ)[:, None] * np.arange(NB)[None, :]) / NE
    co, so, ci, si = np.cos(outer), np.sin(outer), np.cos(inner), np.sin(inner)
    d1 = np.block([[co.T, so.T], [-so.T, co.T]])
    d2 = np.block([[ci, -si], [si, ci]])
    e2 = np.block([[ci, si], [-si, ci]])
    polar_scale, sigma_scale = NE**-1.5, -(float(NE) ** -2)
    e1p = polar_scale * np.block([[-so, -co], [co, -so]])
    e1s = sigma_scale * np.block([[co, -so], [so, co]])
    out = []
    for table in (d1, d2, e2, e1p, e1s):
        out.extend(halves(table))
    out.append(np.cos(twist).astype(np.float32))
    out.append(np.sin(twist).astype(np.float32))
    return tuple(out)


def split(x):
    high = x.astype(BF16)
    return high, (x - high.astype(F32)).astype(BF16)


def dot(a, b):
    return lax.dot_general(a, b, (((1,), (0,)), ((), ())), preferred_element_type=F32)


def dot3(a, b):
    return dot(a[0], b[0]) + (dot(a[0], b[1]) + dot(a[1], b[0]))


def interleave(first, second):
    low = jnp.concatenate([first[:, :KK], second[:, :KK]], axis=1)
    high = jnp.concatenate([first[:, KK:], second[:, KK:]], axis=1)
    return low, high


def pack_kernel(z_ref, lesser, greater, *outs):
    for d in range(NZ):
        start = pl.multiple_of(lax.rem(z_ref[0] + d, NZ) * 128, 128)
        for g, ref in enumerate((lesser, greater)):
            real = ref[0, pl.ds(start, 128), :].reshape(16, 8, 128)
            imag = ref[1, pl.ds(start, 128), :].reshape(16, 8, 128)
            even, odd = interleave(real, imag)
            if len(outs) == 1:
                outs[0][:, 0, d, g] = even
                outs[0][:, 1, d, g] = odd
            else:
                outs[d][:, 0, g] = even
                outs[d][:, 1, g] = odd


def pack(z, lesser, greater, chunk, joined):
    half = pl.BlockSpec((2, 1024, 128), lambda i, z_ref: (0, chunk, 0))
    if joined:
        shapes = [(16, 2, NZ, 2, 8, 128)]
    else:
        shapes = [(16, 2, 2, 8, 128)] * NZ
    outs = pl.pallas_call(
        pack_kernel,
        out_shape=[jax.ShapeDtypeStruct(s, F32) for s in shapes],
        grid_spec=pltpu.PrefetchScalarGridSpec(
            num_scalar_prefetch=1,
            grid=(1,),
            in_specs=[half, half],
            out_specs=[pl.BlockSpec(s, lambda i, z_ref, n=len(s): (0,) * n) for s in shapes],
        ),
        compiler_params=pltpu.CompilerParams(vmem_limit_bytes=LIMIT),
        cost_estimate=pl.CostEstimate(flops=1 << 20, bytes_accessed=1 << 22, transcendentals=0),
        name="pack",
    )(z, lesser, greater)
    if joined:
        return outs[0].reshape(NU, NZ, 16, 128)
    return [o.reshape(NU, 16, 128) for o in outs]


def merge_kernel(*refs):
    sem = refs[-1]
    out = refs[-2]
    copies = [pltpu.make_async_copy(refs[d], out.at[:, d], sem.at[d]) for d in range(NZ)]
    for copy in copies:
        copy.start()
    for copy in copies:
        copy.wait()


def merge(blocks):
    return pl.pallas_call(
        merge_kernel,
        out_shape=jax.ShapeDtypeStruct((NU, NZ, 16, 128), F32),
        in_specs=[HBM] * NZ,
        out_specs=HBM,
        scratch_shapes=[pltpu.SemaphoreType.DMA((NZ,))],
        cost_estimate=pl.CostEstimate(flops=0, bytes_accessed=1 << 22, transcendentals=0),
        name="merge",
    )(*blocks)


def convolve_kernel(joined_in, joined_out, *refs):
    n_in = 1 if joined_in else NZ
    n_out = 1 if joined_out else NZ
    z_ref, weights = refs[:2]
    ins = refs[2 : 2 + n_in]
    consts = refs[2 + n_in : 14 + n_in]
    outs = refs[14 + n_in : 14 + n_in + n_out]
    xin, yout, sem = refs[14 + n_in + n_out :]
    d1, d2, e2, e1p, e1s = [(consts[2 * i][...], consts[2 * i + 1][...]) for i in range(5)]
    cos, sin = consts[10][...], consts[11][...]
    z = z_ref[0]

    copies = []
    for d in range(NZ):
        place = pl.ds(lax.rem(z + (NZ - d), NZ) * NU, NU)
        source = ins[0].at[:, d] if joined_in else ins[d]
        copies.append(pltpu.make_async_copy(source, xin.at[place], sem.at[d]))
    for copy in copies:
        copy.start()
    for copy in copies:
        copy.wait()

    rows_in = xin.reshape(NZ * NU * 16, 128)
    rows_out = yout.reshape(NZ * NU * 16, 128)

    def step(kk, carry):
        turned = []
        for g in range(2):
            for r in range(4):
                parts = []
                for c in range(2):
                    for zh in range(2):
                        base = (zh * 4 + r) * NU * 16 + g * 8 + c * KK + kk
                        parts.append(rows_in[pl.ds(base, NU, stride=16), :])
                y = dot3(d1, split(jnp.concatenate(parts, axis=0)))
                yr, yi = y[:NJ], y[NJ:]
                turned.append(
                    jnp.concatenate([yr * cos + yi * sin, yi * cos - yr * sin], axis=1)
                )
        spec = dot3(split(jnp.concatenate(turned, axis=0)), d2)
        lr, li = spec[:256, :NB], spec[:256, NB:]
        gr, gi = spec[256:, :NB], spec[256:, NB:]
        cr = lr * gr + li * gi
        ci = li * gr - lr * gi
        wr, wi = [], []
        for r in range(4):
            own = weights[r * 8 + kk]
            side = weights[r * 8 + KK + kk]
            for source, dest in ((cr, wr), (ci, wi)):
                rows = [source[q * NJ : (q + 1) * NJ] for q in (r - 1, r + 1) if 0 <= q < 4]
                beside = rows[0] if len(rows) == 1 else rows[0] + rows[1]
                dest.append(own * source[r * NJ : (r + 1) * NJ] + side * beside)
        wr, wi = jnp.concatenate(wr, axis=0), jnp.concatenate(wi, axis=0)
        vr = lr * wr - li * wi
        vi = lr * wi + li * wr
        both = jnp.concatenate(
            [jnp.concatenate([cr, ci], axis=1), jnp.concatenate([vr, vi], axis=1)], axis=0
        )
        back = dot3(split(both), e2)
        for o in range(2):
            for r in range(4):
                part = back[(o * 4 + r) * NJ : (o * 4 + r + 1) * NJ]
                ar, ai = part[:, :NB], part[:, NB:]
                turn = jnp.concatenate([ar * cos - ai * sin, ai * cos + ar * sin], axis=0)
                done = dot3((e1p, e1s)[o], split(turn))
                for c in range(2):
                    for zh in range(2):
                        base = (zh * 4 + r) * NU * 16 + o * 8 + c * KK + kk
                        at = (c * 2 + zh) * NU
                        rows_out[pl.ds(base, NU, stride=16), :] = done[at : at + NU]
        return carry

    lax.fori_loop(0, KK, step, 0)

    copies = []
    for d in range(NZ):
        place = pl.ds(lax.rem(z + d, NZ) * NU, NU)
        dest = outs[0].at[:, d] if joined_out else outs[d]
        copies.append(pltpu.make_async_copy(yout.at[place], dest, sem.at[d]))
    for copy in copies:
        copy.start()
    for copy in copies:
        copy.wait()


def convolve(z, weights, ins, joined_out):
    consts = [jnp.asarray(t) for t in tables()]
    if joined_out:
        shapes = [(NU, NZ, 16, 128)]
    else:
        shapes = [(NU, 16, 128)] * NZ
    outs = pl.pallas_call(
        functools.partial(convolve_kernel, len(ins) == 1, joined_out),
        out_shape=[jax.ShapeDtypeStruct(s, F32) for s in shapes],
        in_specs=[SMEM, SMEM] + [HBM] * len(ins) + [VMEM] * len(consts),
        out_specs=[HBM] * len(shapes),
        scratch_shapes=[
            pltpu.VMEM((NZ * NU, 16, 128), F32),
            pltpu.VMEM((NZ * NU, 16, 128), F32),
            pltpu.SemaphoreType.DMA((NZ,)),
        ],
        compiler_params=pltpu.CompilerParams(vmem_limit_bytes=LIMIT),
        cost_estimate=pl.CostEstimate(flops=6 * 10**9, bytes_accessed=1 << 22, transcendentals=0),
        name="convolve",
    )(z, weights, *ins, *consts)
    return outs


def unpack_kernel(n_in, n_old, z_ref, *refs):
    ins = refs[:n_in]
    outs = refs[n_in + n_old :]
    for d in range(NZ):
        start = pl.multiple_of(lax.rem(z_ref[0] + (NZ - d), NZ) * 128, 128)
        for o in range(2):
            if n_in == 1:
                even, odd = ins[0][:, 0, d, o], ins[0][:, 1, d, o]
            else:
                even, odd = ins[d][:, 0, o], ins[d][:, 1, o]
            real, imag = interleave(even, odd)
            outs[o][0, pl.ds(start, 128), :] = real.reshape(128, 128)
            outs[o][1, pl.ds(start, 128), :] = imag.reshape(128, 128)


def unpack(z, ins, chunk, old):
    if len(ins) == 1:
        ins = [ins[0].reshape(16, 2, NZ, 2, 8, 128)]
    else:
        ins = [x.reshape(16, 2, 2, 8, 128) for x in ins]
    half = pl.BlockSpec((2, 1024, 128), lambda i, z_ref: (0, chunk, 0))
    whole = [pl.BlockSpec(x.shape, lambda i, z_ref, n=x.ndim: (0,) * n) for x in ins]
    return pl.pallas_call(
        functools.partial(unpack_kernel, len(ins), len(old)),
        out_shape=[jax.ShapeDtypeStruct((2, 2048, 128), F32)] * 2,
        grid_spec=pltpu.PrefetchScalarGridSpec(
            num_scalar_prefetch=1,
            grid=(1,),
            in_specs=whole + [HBM] * len(old),
            out_specs=[half, half],
        ),
        input_output_aliases={1 + len(ins) + i: i for i in range(len(old))},
        compiler_params=pltpu.CompilerParams(vmem_limit_bytes=LIMIT),
        cost_estimate=pl.CostEstimate(flops=1 << 20, bytes_accessed=1 << 22, transcendentals=0),
        name="unpack",
    )(z, *ins, *old)


def round_ring(blocks):
    out = [blocks[0]]
    for d in range(1, NZ):
        out.append(lax.ppermute(blocks[d], RING, [(i, (i + d) % NZ) for i in range(NZ)]))
    return out


def over_plane(x):
    return lax.all_to_all(x, PLANE, split_axis=0, concat_axis=0, tiled=True)


def apart(x):
    return [x[:, d] for d in range(NZ)]


def shards(green_lesser, green_greater, screen, couple):
    z = lax.axis_index(RING).astype(jnp.int32)
    u = lax.axis_index(PLANE).astype(jnp.int32)
    z1 = z.reshape(1)
    gains = lax.all_gather(jnp.stack([screen, couple]), "zl")
    weights = [
        lax.dynamic_slice(gains, (0, 0, q * 1024 + z * 128 + u * KK), (4, 2, KK)).reshape(-1)
        for q in range(2)
    ]
    first = round_ring(pack(z1, green_lesser, green_greater, 0, False))
    second = apart(over_plane(pack(z1, green_lesser, green_greater, 1, True)))
    second = round_ring(second)
    first = over_plane(merge(first))
    first = convolve(z1, weights[0], [first], False)
    first = round_ring(first)
    second = convolve(z1, weights[1], second, True)[0]
    second = round_ring(apart(over_plane(second)))
    first = over_plane(merge(first))
    done = unpack(z1, [first], 0, [])
    polar, sigma = unpack(z1, second, 1, done)
    return polar, sigma


def solution(mesh):
    named = Mesh(mesh.devices.reshape(SIZES), AXES)
    placed = P(None, "zl", ("x", "zh", "y", "c"))
    return jax.shard_map(
        shards,
        mesh=named,
        in_specs=(placed, placed, P("zl"), P("zl")),
        out_specs=(placed, placed),
        check_vma=False,
    )
```

```python
import functools
import math

import jax
import jax.numpy as jnp
import ml_dtypes
import numpy as np
from jax import lax
from jax.experimental import pallas as pl
from jax.experimental.pallas import tpu as pltpu
from jax.sharding import Mesh
from jax.sharding import PartitionSpec as P

SIZES = (4, 2, 4, 2, 4)
AXES = ("x", "zh", "y", "c", "zl")
RING = ("zh", "zl")
PLANE = ("x", "y", "c")
NZ, NU = 8, 32
NXY = NU // 2
STEPS = (1, 2, 3)
BLOCK = (NU, 16, 128)
NJ, NB = 64, 128
NE = NJ * NB
KK = 4
F32, BF16 = jnp.float32, jnp.bfloat16
HBM = pl.BlockSpec(memory_space=pl.ANY)
VMEM = pl.BlockSpec(memory_space=pltpu.VMEM)
SMEM = pl.BlockSpec(memory_space=pltpu.SMEM)
LIMIT = 58 * 1024 * 1024


def halves(table):
    high = table.astype(np.float32).astype(ml_dtypes.bfloat16)
    low = (table - high.astype(np.float64)).astype(np.float32).astype(ml_dtypes.bfloat16)
    return high, low


@functools.lru_cache(maxsize=1)
def tables():
    zh, u = np.meshgrid(np.arange(2), np.arange(NU), indexing="ij")
    j = ((u // 8) * 16 + zh * 8 + u % 8).reshape(-1)
    outer = 2 * math.pi * (j[:, None] * np.arange(NJ)[None, :] % NJ) / NJ
    inner = 2 * math.pi * (np.arange(NB)[:, None] * np.arange(NB)[None, :] % NB) / NB
    twist = 2 * math.pi * (np.arange(NJ)[:, None] * np.arange(NB)[None, :]) / NE
    co, so, ci, si = np.cos(outer), np.sin(outer), np.cos(inner), np.sin(inner)
    d1 = np.block([[co.T, so.T], [-so.T, co.T]])
    d2 = np.block([[ci, -si], [si, ci]])
    e2 = np.block([[ci, si], [-si, ci]])
    polar_scale, sigma_scale = NE**-1.5, -(float(NE) ** -2)
    e1p = polar_scale * np.block([[-so, -co], [co, -so]])
    e1s = sigma_scale * np.block([[co, -so], [so, co]])
    out = []
    for table in (d1, d2, e2, e1p, e1s):
        out.extend(halves(table))
    out.append(np.cos(twist).astype(np.float32))
    out.append(np.sin(twist).astype(np.float32))
    return tuple(out)


def split(x):
    high = x.astype(BF16)
    return high, (x - high.astype(F32)).astype(BF16)


def dot(a, b):
    return lax.dot_general(a, b, (((1,), (0,)), ((), ())), preferred_element_type=F32)


def dot3(a, b):
    return dot(a[0], b[0]) + (dot(a[0], b[1]) + dot(a[1], b[0]))


def interleave(first, second):
    low = jnp.concatenate([first[:, :KK], second[:, :KK]], axis=1)
    high = jnp.concatenate([first[:, KK:], second[:, KK:]], axis=1)
    return low, high


def around(z, shift):
    return lax.rem(z + (shift + NZ), NZ)


def whole(shape):
    return pl.BlockSpec(shape, lambda i, *_: (0,) * len(shape))


def local_call(kernel, scalars, ins, in_specs, after, shapes, out_specs, name, aliases=None):
    count = len(ins)
    return pl.pallas_call(
        lambda *refs: kernel(
            refs[:1], refs[1 : 1 + count], refs[1 + count + len(after) :]
        ),
        out_shape=[jax.ShapeDtypeStruct(s, F32) for s in shapes],
        grid_spec=pltpu.PrefetchScalarGridSpec(
            num_scalar_prefetch=1,
            grid=(1,),
            in_specs=list(in_specs) + [HBM] * len(after),
            out_specs=out_specs,
        ),
        input_output_aliases=aliases or {},
        compiler_params=pltpu.CompilerParams(vmem_limit_bytes=LIMIT),
        cost_estimate=pl.CostEstimate(flops=1 << 20, bytes_accessed=1 << 22, transcendentals=0),
        name=name,
    )(scalars, *ins, *after)


def blocks_of(lesser, greater, zd):
    start = pl.multiple_of(zd * 128, 128)
    for g, ref in enumerate((lesser, greater)):
        real = ref[0, pl.ds(start, 128), :].reshape(NXY, 8, 128)
        imag = ref[1, pl.ds(start, 128), :].reshape(NXY, 8, 128)
        yield g, *interleave(real, imag)


def pack_ring_kernel(scalars, ins, outs):
    lesser, greater, screen, couple = ins
    own, far, keep, give, gains = outs
    z, sign = scalars[0][0], scalars[0][1]
    targets = [(own, 0), (far, 4)]
    targets += [(keep.at[d - 1], sign * d) for d in STEPS]
    targets += [(give.at[d - 1], -sign * d) for d in STEPS]
    for dest, shift in targets:
        for g, even, odd in blocks_of(lesser, greater, around(z, shift)):
            dest[:, 0, g] = even
            dest[:, 1, g] = odd
    for d in range(4):
        zd = around(z, sign * d)
        rows = [ref[pl.ds(zd + q * NZ, 1), :] for ref in (screen, couple) for q in range(2)]
        gains[d] = jnp.concatenate(rows + rows, axis=0)


def pack_ring(scalars, lesser, greater, screen, couple):
    half = pl.BlockSpec((2, 1024, 128), lambda i, *_: (0, 0, 0))
    small = whole((16, 128))
    one = (NXY, 2, 2, 8, 128)
    shapes = [one, one, (3, *one), (3, *one), (4, 8, 128)]
    own, far, keep, give, gains = local_call(
        pack_ring_kernel,
        scalars,
        [lesser, greater, screen.reshape(16, 128), couple.reshape(16, 128)],
        [half, half, small, small],
        [],
        shapes,
        [whole(s) for s in shapes],
        "pack_ring",
    )
    return own.reshape(BLOCK), far.reshape(BLOCK), keep.reshape(3, *BLOCK), give.reshape(3, *BLOCK), gains


def pack_plane_kernel(scalars, ins, outs):
    lesser, greater = ins
    out = outs[0]
    z = scalars[0][0]
    for shift in range(-3, 5):
        for g, even, odd in blocks_of(lesser, greater, around(z, shift)):
            if shift in (0, 4):
                out[:, 0, shift // 4, g] = even
                out[:, 1, shift // 4, g] = odd
            elif shift > 0:
                out[:, 0, 2 * shift, g] = even
                out[:, 0, 2 * shift + 1, g] = odd
            else:
                out[:, 1, -2 * shift, g] = odd
                out[:, 1, -2 * shift + 1, g] = even


def pack_plane(scalars, lesser, greater, after):
    half = pl.BlockSpec((2, 1024, 128), lambda i, *_: (0, 1, 0))
    shape = (NXY, 2, NZ, 2, 8, 128)
    (out,) = local_call(
        pack_plane_kernel, scalars, [lesser, greater], [half, half], after, [shape], [whole(shape)], "pack_plane"
    )
    return out.reshape(NU, NZ, 16, 128)


def merge_kernel(scalars, ins, outs):
    out = outs[0]
    out[:, 0] = ins[0][...]
    out[:, 1] = ins[1][...]
    for d in STEPS:
        for m in range(2):
            out[:, 2 * d + m] = ins[1 + d][m * 64 : m * 64 + 64].reshape(BLOCK)


def merge(scalars, own, far, paid, after):
    ins = [own, far] + paid
    out = (NU, NZ, 16, 128)
    return local_call(
        merge_kernel,
        scalars,
        ins,
        [whole(x.shape) for x in ins],
        after,
        [out],
        [whole(out)],
        "merge",
    )[0]


def fan_kernel(scalars, ins, outs):
    outs[0][...] = ins[0][:, 1]
    for d in STEPS:
        for m in range(2):
            outs[d][:, m] = ins[0][:, 2 * d + m]


def fan(scalars, joined, after):
    shapes = [BLOCK] + [(NU, 2, 16, 128)] * 3
    out = local_call(
        fan_kernel, scalars, [joined], [whole(joined.shape)], after, shapes, [whole(s) for s in shapes], "fan"
    )
    return out[0], list(out[1:])


def convolve_kernel(joined_in, joined_out, chunk, n_after, *refs):
    n_in = 1 if joined_in else 6
    n_out = 1 if joined_out else 4
    refs = list(refs)
    scalars, weights = refs[:2]
    ins = refs[2 : 2 + n_in]
    tabs = refs[2 + n_in : 14 + n_in]
    outs = refs[14 + n_in + n_after : 14 + n_in + n_after + n_out]
    xin, yout, sem, tab_sem = refs[14 + n_in + n_after + n_out :][:4]
    held = refs[18 + n_in + n_after + n_out :]
    z, sign = scalars[0], scalars[1]

    tab_copies = [pltpu.make_async_copy(t, h, tab_sem.at[i]) for i, (t, h) in enumerate(zip(tabs, held))]
    x_at = xin.at[: NZ * NU].reshape(NZ, NXY, 2, 16, 128)
    y_at = yout.at[: NZ * NU].reshape(NZ, NXY, 2, 16, 128)

    def joined_places(direction):
        for c in range(2):
            way = direction * (1 - 2 * c)
            yield c, 0, z, c
            yield c, 1, around(z, 4), c
            for d in STEPS:
                for m in range(2):
                    yield c, 2 * d + m, around(z, way * d), c ^ m

    pairs = []
    if joined_in:
        source = ins[0].reshape(NXY, 2, NZ, 16, 128)
        for c, slot, zs, core in joined_places(-1):
            pairs.append((source.at[:, c, slot], x_at.at[zs, :, core]))
    else:
        own, far, got = ins[0], ins[1], ins[5]
        pairs.append((own.at[:, 0], xin.at[pl.ds(z * NU, NU)]))
        pairs.append((far, xin.at[pl.ds(around(z, 4) * NU, NU)]))
        for d in STEPS:
            pairs.append((ins[1 + d].at[:, 0], xin.at[pl.ds(around(z, -sign * d) * NU, NU)]))
            pairs.append((got.at[d - 1], xin.at[pl.ds(around(z, sign * d) * NU, NU)]))
    copies = [pltpu.make_async_copy(s, t, sem.at[i]) for i, (s, t) in enumerate(pairs)]
    for copy in copies + tab_copies:
        copy.start()
    for copy in copies + tab_copies:
        copy.wait()

    d1, d2, e2, e1p, e1s = [(held[2 * i][...], held[2 * i + 1][...]) for i in range(5)]
    cos, sin = held[10][...], held[11][...]
    rows_in = xin.reshape((NZ * NU + 1) * 16, 128)
    rows_out = yout.reshape((NZ * NU + 1) * 16, 128)

    def step(kk, carry):
        turned = []
        for g in range(2):
            for r in range(4):
                parts = []
                for c in range(2):
                    for zh in range(2):
                        base = (zh * 4 + r) * NU * 16 + g * 8 + c * KK + kk
                        parts.append(rows_in[pl.ds(base, NU, stride=16), :])
                y = dot3(d1, split(jnp.concatenate(parts, axis=0)))
                yr, yi = y[:NJ], y[NJ:]
                turned.append(jnp.concatenate([yr * cos + yi * sin, yi * cos - yr * sin], axis=1))
        spec = dot3(split(jnp.concatenate(turned, axis=0)), d2)
        lr, li = spec[:256, :NB], spec[:256, NB:]
        gr, gi = spec[256:, :NB], spec[256:, NB:]
        cr = lr * gr + li * gi
        ci = li * gr - lr * gi
        wr, wi = [], []
        for r in range(4):
            d = lax.rem((z + (NZ - r)) * sign + 4 * NZ, 4)
            own_gain = weights[d * 16 + chunk * KK + kk]
            side_gain = weights[d * 16 + 8 + chunk * KK + kk]
            for source, dest in ((cr, wr), (ci, wi)):
                rows = [source[q * NJ : (q + 1) * NJ] for q in (r - 1, r + 1) if 0 <= q < 4]
                beside = rows[0] if len(rows) == 1 else rows[0] + rows[1]
                dest.append(own_gain * source[r * NJ : (r + 1) * NJ] + side_gain * beside)
        wr, wi = jnp.concatenate(wr, axis=0), jnp.concatenate(wi, axis=0)
        vr = lr * wr - li * wi
        vi = lr * wi + li * wr
        both = jnp.concatenate(
            [jnp.concatenate([cr, ci], axis=1), jnp.concatenate([vr, vi], axis=1)], axis=0
        )
        back = dot3(split(both), e2)
        for o in range(2):
            for r in range(4):
                part = back[(o * 4 + r) * NJ : (o * 4 + r + 1) * NJ]
                ar, ai = part[:, :NB], part[:, NB:]
                turn = jnp.concatenate([ar * cos - ai * sin, ai * cos + ar * sin], axis=0)
                done = dot3((e1p, e1s)[o], split(turn))
                for c in range(2):
                    for zh in range(2):
                        base = (zh * 4 + r) * NU * 16 + o * 8 + c * KK + kk
                        at = (c * 2 + zh) * NU
                        rows_out[pl.ds(base, NU, stride=16), :] = done[at : at + NU]
        return carry

    lax.fori_loop(0, KK, step, 0)

    pairs = []
    if joined_out:
        dest = outs[0].reshape(NXY, 2, NZ, 16, 128)
        for c, slot, zd, core in joined_places(1):
            pairs.append((y_at.at[zd, :, core], dest.at[:, c, slot]))
    else:
        own, far, keep, give = outs
        pairs.append((yout.at[pl.ds(z * NU, NU)], own))
        pairs.append((yout.at[pl.ds(around(z, 4) * NU, NU)], far))
        for d in STEPS:
            pairs.append((yout.at[pl.ds(around(z, sign * d) * NU, NU)], keep.at[d - 1]))
            pairs.append((yout.at[pl.ds(around(z, -sign * d) * NU, NU)], give.at[d - 1]))
    copies = [pltpu.make_async_copy(s, t, sem.at[i]) for i, (s, t) in enumerate(pairs)]
    for copy in copies:
        copy.start()
    for copy in copies:
        copy.wait()


def convolve(scalars, weights, ins, joined_out, chunk, after):
    consts = [jnp.asarray(t) for t in tables()]
    if joined_out:
        shapes = [(NU, NZ, 16, 128)]
    else:
        shapes = [BLOCK, BLOCK, (3, *BLOCK), (3, *BLOCK)]
    return pl.pallas_call(
        functools.partial(convolve_kernel, len(ins) == 1, joined_out, chunk, len(after)),
        out_shape=[jax.ShapeDtypeStruct(s, F32) for s in shapes],
        in_specs=[SMEM, SMEM] + [HBM] * (len(ins) + len(consts) + len(after)),
        out_specs=[HBM] * len(shapes),
        scratch_shapes=[
            pltpu.VMEM((NZ * NU + 1, 16, 128), F32),
            pltpu.VMEM((NZ * NU + 1, 16, 128), F32),
            pltpu.SemaphoreType.DMA((2 * NZ,)),
            pltpu.SemaphoreType.DMA((12,)),
        ]
        + [pltpu.VMEM(t.shape, t.dtype) for t in consts],
        compiler_params=pltpu.CompilerParams(vmem_limit_bytes=LIMIT),
        cost_estimate=pl.CostEstimate(flops=6 * 10**9, bytes_accessed=1 << 22, transcendentals=0),
        name="convolve",
    )(scalars, weights, *ins, *consts, *after)


def unpack_kernel(joined, scalars, ins, outs):
    z, sign = scalars[0][0], scalars[0][1]

    def put(shift, even, odd):
        start = pl.multiple_of(around(z, shift) * 128, 128)
        for o in range(2):
            real, imag = interleave(even[o], odd[o])
            outs[o][0, pl.ds(start, 128), :] = real.reshape(128, 128)
            outs[o][1, pl.ds(start, 128), :] = imag.reshape(128, 128)

    if joined:
        v = ins[0]
        for shift in range(-3, 5):
            if shift in (0, 4):
                even, odd = (0, shift // 4), (1, shift // 4)
            elif shift < 0:
                even, odd = (0, -2 * shift), (0, -2 * shift + 1)
            else:
                even, odd = (1, 2 * shift + 1), (1, 2 * shift)
            put(shift, [v[:, *even, o] for o in range(2)], [v[:, *odd, o] for o in range(2)])
    else:
        own, far, *paid, got = ins
        put(0, *[[own[:, c, 0, o] for o in range(2)] for c in range(2)])
        put(4, *[[far[:, c, o] for o in range(2)] for c in range(2)])
        for d in STEPS:
            put(-sign * d, *[[paid[d - 1][:, c, 0, o] for o in range(2)] for c in range(2)])
            put(sign * d, *[[got[d - 1, :, c, o] for o in range(2)] for c in range(2)])


def unpack(scalars, ins, chunk, old):
    half = pl.BlockSpec((2, 1024, 128), lambda i, *_: (0, chunk, 0))
    joined = len(ins) == 1
    if joined:
        ins = [ins[0].reshape(NXY, 2, NZ, 2, 8, 128)]
    else:
        own, far, *paid, got = ins
        ins = [own.reshape(NXY, 2, NZ, 2, 8, 128), far.reshape(NXY, 2, 2, 8, 128)]
        ins += [x.reshape(NXY, 2, 2, 2, 8, 128) for x in paid]
        ins.append(got.reshape(3, NXY, 2, 2, 8, 128))
    return local_call(
        functools.partial(unpack_kernel, joined),
        scalars,
        ins,
        [whole(x.shape) for x in ins],
        old,
        [(2, 2048, 128)] * 2,
        [half, half],
        "unpack",
        {1 + len(ins) + i: i for i in range(len(old))},
    )


def to_ring(x, shift):
    moves = []
    for zh in range(2):
        for c in range(2):
            for zl in range(4):
                to = (zh * 4 + zl + (1 - 2 * c) * shift) % NZ
                moves.append((zh * 8 + c * 4 + zl, (to // 4) * 8 + c * 4 + to % 4))
    return lax.ppermute(x, ("zh", "c", "zl"), moves)


def to_far(x):
    return lax.ppermute(x, RING, [(i, (i + 4) % NZ) for i in range(NZ)])


def to_core(x):
    return lax.ppermute(x, "c", [(0, 1), (1, 0)])


def over_plane(x):
    return lax.all_to_all(x, PLANE, split_axis=0, concat_axis=0, tiled=True)


def shards(green_lesser, green_greater, screen, couple):
    z = lax.axis_index(RING).astype(jnp.int32)
    u = lax.axis_index(PLANE).astype(jnp.int32)
    scalars = jnp.stack([z, 1 - 2 * lax.rem(u, 2)])
    own, far, keep, give, gains = pack_ring(scalars, green_lesser, green_greater, screen, couple)
    far = to_far(far)
    got = to_core(give)
    rows = [
        jnp.concatenate([keep[d - 1].reshape(512, 128), got[d - 1].reshape(512, 128), gains[d]], axis=0)
        for d in STEPS
    ]
    second = over_plane(pack_plane(scalars, green_lesser, green_greater, rows))
    rows = [to_ring(x, d) for d, x in zip(STEPS, rows)]
    paid = [x.reshape(129, 8, 128) for x in rows]

    far2, paid2 = fan(scalars, second, [])
    order = [paid2[0]]
    far2 = to_far(far2)
    paid2 = [to_ring(x, d) for d, x in zip(STEPS, paid2)]

    first = merge(scalars, own, far, paid, order)
    gains = jnp.stack([gains[0, :4]] + [x[1024:1028] for x in rows])
    weights = lax.dynamic_slice(gains, (0, 0, u * KK), (4, 4, KK)).reshape(-1)
    first = over_plane(first)
    own, far, keep, give = convolve(scalars, weights, [first], False, 0, [])
    far = to_far(far)
    got = to_core(give)
    paid = [jnp.concatenate([keep[d - 1], got[d - 1]], axis=0) for d in STEPS]
    order = [paid[0]]
    paid = [to_ring(x, d).reshape(128, 8, 128) for d, x in zip(STEPS, paid)]

    got2 = to_core(jnp.stack([x[:, 1] for x in paid2]))
    (second,) = convolve(scalars, weights, [second, far2, *paid2, got2], True, 1, order)
    second = over_plane(second)
    far2, paid2 = fan(scalars, second, [])
    order = [paid2[0]]
    far2 = to_far(far2)
    paid2 = [to_ring(x, d) for d, x in zip(STEPS, paid2)]

    first = over_plane(merge(scalars, own, far, paid, order))
    done = unpack(scalars, [first], 0, [])
    got2 = to_core(jnp.stack([x[:, 1] for x in paid2]))
    polar, sigma = unpack(scalars, [second, far2, *paid2, got2], 1, done)
    return polar, sigma


def solution(mesh):
    named = Mesh(mesh.devices.reshape(SIZES), AXES)
    placed = P(None, "zl", ("x", "zh", "y", "c"))
    return jax.shard_map(
        shards,
        mesh=named,
        in_specs=(placed, placed, P("zl"), P("zl")),
        out_specs=(placed, placed),
        check_vma=False,
    )
```

```python
import functools
import math

import jax
import jax.numpy as jnp
import ml_dtypes
import numpy as np
from jax import lax
from jax.experimental import pallas as pl
from jax.experimental.pallas import tpu as pltpu
from jax.sharding import Mesh
from jax.sharding import PartitionSpec as P

SIZES = (4, 2, 4, 2, 4)
AXES = ("x", "zh", "y", "c", "zl")
RING = ("zh", "zl")
PLANE = ("x", "y", "c")
NZ, NU = 8, 32
NXY = NU // 2
STEPS = (1, 2, 3)
PARTS = 1
BLOCK = (NU, 16, 128)
NJ, NB = 64, 128
NE = NJ * NB
KK = 4
F32, BF16 = jnp.float32, jnp.bfloat16
HBM = pl.BlockSpec(memory_space=pl.ANY)
VMEM = pl.BlockSpec(memory_space=pltpu.VMEM)
SMEM = pl.BlockSpec(memory_space=pltpu.SMEM)
LIMIT = 20 * 1024 * 1024
FULL = 58 * 1024 * 1024
LONG = 2 * 10**11


def halves(table):
    high = table.astype(np.float32).astype(ml_dtypes.bfloat16)
    low = (table - high.astype(np.float64)).astype(np.float32).astype(ml_dtypes.bfloat16)
    return high, low


@functools.lru_cache(maxsize=1)
def tables():
    zh, u = np.meshgrid(np.arange(2), np.arange(NU), indexing="ij")
    j = ((u // 8) * 16 + zh * 8 + u % 8).reshape(-1)
    outer = 2 * math.pi * (j[:, None] * np.arange(NJ)[None, :] % NJ) / NJ
    inner = 2 * math.pi * (np.arange(NB)[:, None] * np.arange(NB)[None, :] % NB) / NB
    twist = 2 * math.pi * (np.arange(NJ)[:, None] * np.arange(NB)[None, :]) / NE
    co, so, ci, si = np.cos(outer), np.sin(outer), np.cos(inner), np.sin(inner)
    d1 = np.block([[co.T, so.T], [-so.T, co.T]])
    d2 = np.block([[ci, -si], [si, ci]])
    e2 = np.block([[ci, si], [-si, ci]])
    polar_scale, sigma_scale = NE**-1.5, -(float(NE) ** -2)
    e1p = polar_scale * np.block([[-so, -co], [co, -so]])
    e1s = sigma_scale * np.block([[co, -so], [so, co]])
    products = [np.concatenate(halves(table), axis=1) for table in (d1, e1p, e1s)]
    for table in (d2, e2):
        products.extend(halves(table))
    turns = np.concatenate([np.cos(twist), np.sin(twist)], axis=1).astype(np.float32)
    return np.concatenate(products, axis=0), turns


def split(x):
    high = x.astype(BF16)
    return high, (x - high.astype(F32)).astype(BF16)


def dot(a, b):
    return lax.dot_general(a, b, (((1,), (0,)), ((), ())), preferred_element_type=F32)


def dot3(a, b):
    return dot(a[0], b[0]) + (dot(a[0], b[1]) + dot(a[1], b[0]))


def dot_pair(table, first, second):
    high, low = split(jnp.concatenate([first, second], axis=1))
    out = dot(table, jnp.concatenate([high, high], axis=0)) + dot(table[:, :128], low)
    return out[:, :NB], out[:, NB:]


def interleave(first, second):
    low = jnp.concatenate([first[:, :KK], second[:, :KK]], axis=1)
    high = jnp.concatenate([first[:, KK:], second[:, KK:]], axis=1)
    return low, high


def around(z, shift):
    return lax.rem(z + (shift + NZ), NZ)


def whole(shape):
    return pl.BlockSpec(shape, lambda i, *_: (0,) * len(shape))


def part(shape, dim, at=()):
    block, fixed = list(shape), [0] * len(shape)
    block[dim] //= PARTS
    for where, length, index in at:
        block[where], fixed[where] = length, index
    return pl.BlockSpec(
        tuple(block), lambda i, *_: tuple(i if n == dim else f for n, f in enumerate(fixed))
    )


def local_call(
    kernel, scalars, ins, in_specs, after, shapes, out_specs, name, aliases=None, work=0, limit=LIMIT
):
    count = len(ins)
    return pl.pallas_call(
        lambda *refs: kernel(refs[:1], refs[1 : 1 + count], refs[1 + count + len(after) :]),
        out_shape=[jax.ShapeDtypeStruct(s, F32) for s in shapes],
        grid_spec=pltpu.PrefetchScalarGridSpec(
            num_scalar_prefetch=1,
            grid=(PARTS,),
            in_specs=list(in_specs) + [HBM] * len(after),
            out_specs=out_specs,
        ),
        input_output_aliases=aliases or {},
        compiler_params=pltpu.CompilerParams(vmem_limit_bytes=limit),
        cost_estimate=pl.CostEstimate(flops=work, bytes_accessed=0, transcendentals=0),
        name=name,
    )(scalars, *ins, *after)


GRID_IN = (2, 2 * NZ, NXY, 8, 128)


def chunk_part(chunk):
    return part(GRID_IN, 2, [(1, NZ, chunk)])


def blocks_of(lesser, greater, zd):
    for g, ref in enumerate((lesser, greater)):
        yield g, *interleave(ref[0, zd], ref[1, zd])


def pack_ring_kernel(scalars, ins, outs):
    lesser, greater, screen, couple = ins
    own, far, keep, give, gains = outs
    z, sign = scalars[0][0], scalars[0][1]
    targets = [(own, 0), (far, 4)]
    targets += [(keep.at[d - 1], sign * d) for d in STEPS]
    targets += [(give.at[d - 1], -sign * d) for d in STEPS]
    for dest, shift in targets:
        for g, even, odd in blocks_of(lesser, greater, around(z, shift)):
            dest[:, 0, g] = even
            dest[:, 1, g] = odd
    for d in range(4):
        zd = around(z, sign * d)
        rows = [ref[pl.ds(zd + q * NZ, 1), :] for ref in (screen, couple) for q in range(2)]
        gains[d] = jnp.concatenate(rows * 4, axis=0)


def pack_ring(scalars, lesser, greater, screen, couple):
    small = whole((16, 128))
    one = (NXY, 2, 2, 8, 128)
    shapes = [one, one, (3, *one), (3, *one), (4, 16, 128)]
    own, far, keep, give, gains = local_call(
        pack_ring_kernel,
        scalars,
        [lesser.reshape(GRID_IN), greater.reshape(GRID_IN), screen.reshape(16, 128), couple.reshape(16, 128)],
        [chunk_part(0), chunk_part(0), small, small],
        [],
        shapes,
        [part(one, 0), part(one, 0), part((3, *one), 1), part((3, *one), 1), whole((4, 16, 128))],
        "pack_ring",
        limit=FULL,
    )
    return own.reshape(BLOCK), far.reshape(BLOCK), keep.reshape(3, *BLOCK), give.reshape(3, *BLOCK), gains


def pack_plane_kernel(scalars, ins, outs):
    lesser, greater = ins
    out = outs[0]
    z = scalars[0][0]
    for shift in range(-3, 5):
        for g, even, odd in blocks_of(lesser, greater, around(z, shift)):
            if shift in (0, 4):
                out[:, 0, shift // 4, g] = even
                out[:, 1, shift // 4, g] = odd
            elif shift > 0:
                out[:, 0, 2 * shift, g] = even
                out[:, 0, 2 * shift + 1, g] = odd
            else:
                out[:, 1, -2 * shift, g] = odd
                out[:, 1, -2 * shift + 1, g] = even


def pack_plane(scalars, lesser, greater, after):
    shape = (NXY, 2, NZ, 2, 8, 128)
    (out,) = local_call(
        pack_plane_kernel,
        scalars,
        [lesser.reshape(GRID_IN), greater.reshape(GRID_IN)],
        [chunk_part(1), chunk_part(1)],
        after,
        [shape],
        [part(shape, 0)],
        "pack_plane",
        limit=FULL,
    )
    return out.reshape(NU, NZ, 16, 128)


def shuttle(ins, shapes, routes, name, through=None, after=(), work=LONG):
    count, n_after = len(ins), len(after) + (through is not None)
    extra = [] if through is None else [through]

    def kernel(*refs):
        outs = refs[count + n_after :]
        held, in_sem, out_sem = refs[-3:]
        pulls = [
            pltpu.make_async_copy(refs[i].at[a], held.at[n], in_sem.at[n]) for n, (i, a, _, _) in enumerate(routes)
        ]
        pushes = [
            pltpu.make_async_copy(held.at[n], outs[o].at[b], out_sem.at[n]) for n, (_, _, o, b) in enumerate(routes)
        ]
        for copy in pulls:
            copy.start()
        for pull, push in zip(pulls, pushes):
            pull.wait()
            push.start()
        for copy in pushes:
            copy.wait()

    return pl.pallas_call(
        kernel,
        out_shape=[jax.ShapeDtypeStruct(s, F32) for s in shapes + [x.shape for x in extra]],
        in_specs=[HBM] * (count + n_after),
        out_specs=[HBM] * (len(shapes) + len(extra)),
        scratch_shapes=[
            pltpu.VMEM((len(routes), *BLOCK), F32),
            pltpu.SemaphoreType.DMA((len(routes),)),
            pltpu.SemaphoreType.DMA((len(routes),)),
        ],
        input_output_aliases={count: len(shapes)} if extra else {},
        compiler_params=pltpu.CompilerParams(vmem_limit_bytes=LIMIT),
        cost_estimate=pl.CostEstimate(flops=work, bytes_accessed=0, transcendentals=0),
        name=name,
    )(*ins, *extra, *after)


ALL = slice(None)


def merge(own, far, paid):
    ins = [own.reshape(NU, 16, 128), far] + [x.reshape(-1, 16, 128) for x in paid]
    routes = [(0, ALL, 0, (ALL, 0)), (1, ALL, 0, (ALL, 1))]
    for d in STEPS:
        for m in range(2):
            routes.append((1 + d, pl.ds(m * NU, NU), 0, (ALL, 2 * d + m)))
    return shuttle(ins, [(NU, NZ, 16, 128)], routes, "merge")[0]


def give_back(paid, far):
    routes = [(d - 1, 1, 0, d - 1) for d in STEPS]
    return shuttle(paid, [(3, *BLOCK)], routes, "give", after=[far])[0]


def fan(joined, through):
    routes = [(0, (ALL, 1), 0, ALL)]
    for d in STEPS:
        for m in range(2):
            routes.append((0, (ALL, 2 * d + m), d, m))
    out = shuttle([joined], [BLOCK] + [(2, *BLOCK)] * 3, routes, "fan", through=through, work=0)
    return out[0], list(out[1:4]), out[4]


def convolve_kernel(joined_in, joined_out, chunk, n_after, *refs):
    n_in = 1 if joined_in else 6
    n_out = 1 if joined_out else 4
    refs = list(refs)
    scalars, weights = refs[:2]
    ins = refs[2 : 2 + n_in]
    tabs = refs[2 + n_in : 4 + n_in]
    outs = refs[4 + n_in + n_after : 4 + n_in + n_after + n_out]
    xin, yout, sem, tab_sem = refs[4 + n_in + n_after + n_out :][:4]
    held = refs[8 + n_in + n_after + n_out :]
    z, sign = scalars[0], scalars[1]

    tab_copies = [pltpu.make_async_copy(t, h, tab_sem.at[i]) for i, (t, h) in enumerate(zip(tabs, held))]
    x_at = xin.at[: NZ * NU].reshape(NZ, NXY, 2, 16, 128)
    y_at = yout.at[: NZ * NU].reshape(NZ, NXY, 2, 16, 128)

    def joined_places(direction):
        for c in range(2):
            way = direction * (1 - 2 * c)
            yield c, 0, z, c
            yield c, 1, around(z, 4), c
            for d in STEPS:
                for m in range(2):
                    yield c, 2 * d + m, around(z, way * d), c ^ m

    pairs = []
    if joined_in:
        source = ins[0].reshape(NXY, 2, NZ, 16, 128)
        for c, slot, zs, core in joined_places(-1):
            pairs.append((source.at[:, c, slot], x_at.at[zs, :, core]))
    else:
        own, far, got = ins[0], ins[1], ins[5]
        pairs.append((own.at[:, 0], xin.at[pl.ds(z * NU, NU)]))
        pairs.append((far, xin.at[pl.ds(around(z, 4) * NU, NU)]))
        for d in STEPS:
            pairs.append((ins[1 + d].at[0], xin.at[pl.ds(around(z, -sign * d) * NU, NU)]))
            pairs.append((got.at[d - 1], xin.at[pl.ds(around(z, sign * d) * NU, NU)]))
    copies = [pltpu.make_async_copy(s, t, sem.at[i]) for i, (s, t) in enumerate(pairs)]
    for copy in copies + tab_copies:
        copy.start()
    for copy in copies + tab_copies:
        copy.wait()

    products, turns = held
    d1, e1p, e1s = [products[i * 128 : i * 128 + 128] for i in range(3)]
    d2, e2 = [
        (products[i * 512 + 384 : i * 512 + 640], products[i * 512 + 640 : i * 512 + 896]) for i in range(2)
    ]
    cos, sin = turns[:, :NB], turns[:, NB:]
    rows_in = xin.reshape((NZ * NU + 1) * 16, 128)
    rows_out = yout.reshape((NZ * NU + 1) * 16, 128)

    def step(kk, carry):
        turned = []
        for g in range(2):
            for r in (0, 2):
                sides = []
                for row in (r, r + 1):
                    parts = []
                    for c in range(2):
                        for zh in range(2):
                            base = (zh * 4 + row) * NU * 16 + g * 8 + c * KK + kk
                            parts.append(rows_in[pl.ds(base, NU, stride=16), :])
                    sides.append(jnp.concatenate(parts, axis=0))
                for y in dot_pair(d1, *sides):
                    yr, yi = y[:NJ], y[NJ:]
                    turned.append(jnp.concatenate([yr * cos + yi * sin, yi * cos - yr * sin], axis=1))
        spec = dot3(split(jnp.concatenate(turned, axis=0)), d2)
        lr, li = spec[:256, :NB], spec[:256, NB:]
        gr, gi = spec[256:, :NB], spec[256:, NB:]
        cr = lr * gr + li * gi
        ci = li * gr - lr * gi
        wr, wi = [], []
        for r in range(4):
            d = lax.rem((z + (NZ - r)) * sign + 4 * NZ, 4)
            own_gain = weights[d * 16 + chunk * KK + kk]
            side_gain = weights[d * 16 + 8 + chunk * KK + kk]
            for source, dest in ((cr, wr), (ci, wi)):
                rows = [source[q * NJ : (q + 1) * NJ] for q in (r - 1, r + 1) if 0 <= q < 4]
                beside = rows[0] if len(rows) == 1 else rows[0] + rows[1]
                dest.append(own_gain * source[r * NJ : (r + 1) * NJ] + side_gain * beside)
        wr, wi = jnp.concatenate(wr, axis=0), jnp.concatenate(wi, axis=0)
        vr = lr * wr - li * wi
        vi = lr * wi + li * wr
        both = jnp.concatenate(
            [jnp.concatenate([cr, ci], axis=1), jnp.concatenate([vr, vi], axis=1)], axis=0
        )
        back = dot3(split(both), e2)
        for o in range(2):
            for r in (0, 2):
                sides = []
                for row in (r, r + 1):
                    part = back[(o * 4 + row) * NJ : (o * 4 + row + 1) * NJ]
                    ar, ai = part[:, :NB], part[:, NB:]
                    sides.append(jnp.concatenate([ar * cos - ai * sin, ai * cos + ar * sin], axis=0))
                for row, done in zip((r, r + 1), dot_pair((e1p, e1s)[o], *sides)):
                    for c in range(2):
                        for zh in range(2):
                            base = (zh * 4 + row) * NU * 16 + o * 8 + c * KK + kk
                            at = (c * 2 + zh) * NU
                            rows_out[pl.ds(base, NU, stride=16), :] = done[at : at + NU]
        return carry

    lax.fori_loop(0, KK, step, 0, unroll=True)

    pairs = []
    if joined_out:
        dest = outs[0].reshape(NXY, 2, NZ, 16, 128)
        for c, slot, zd, core in joined_places(1):
            pairs.append((y_at.at[zd, :, core], dest.at[:, c, slot]))
    else:
        own, far, keep, give = outs
        pairs.append((yout.at[pl.ds(z * NU, NU)], own))
        pairs.append((yout.at[pl.ds(around(z, 4) * NU, NU)], far))
        for d in STEPS:
            pairs.append((yout.at[pl.ds(around(z, sign * d) * NU, NU)], keep.at[d - 1]))
            pairs.append((yout.at[pl.ds(around(z, -sign * d) * NU, NU)], give.at[d - 1]))
    copies = [pltpu.make_async_copy(s, t, sem.at[i]) for i, (s, t) in enumerate(pairs)]
    for copy in copies:
        copy.start()
    for copy in copies:
        copy.wait()


def convolve(scalars, weights, ins, joined_out, chunk, after):
    consts = [jnp.asarray(t) for t in tables()]
    if joined_out:
        shapes = [(NU, NZ, 16, 128)]
    else:
        shapes = [BLOCK, BLOCK, (3, *BLOCK), (3, *BLOCK)]
    return pl.pallas_call(
        functools.partial(convolve_kernel, len(ins) == 1, joined_out, chunk, len(after)),
        out_shape=[jax.ShapeDtypeStruct(s, F32) for s in shapes],
        in_specs=[SMEM, SMEM] + [HBM] * (len(ins) + len(consts) + len(after)),
        out_specs=[HBM] * len(shapes),
        scratch_shapes=[
            pltpu.VMEM((NZ * NU + 1, 16, 128), F32),
            pltpu.VMEM((NZ * NU + 1, 16, 128), F32),
            pltpu.SemaphoreType.DMA((2 * NZ,)),
            pltpu.SemaphoreType.DMA((2,)),
        ]
        + [pltpu.VMEM(t.shape, t.dtype) for t in consts],
        compiler_params=pltpu.CompilerParams(vmem_limit_bytes=LIMIT),
        cost_estimate=pl.CostEstimate(flops=LONG * chunk, bytes_accessed=0, transcendentals=0),
        name="convolve",
    )(scalars, weights, *ins, *consts, *after)


def unpack_kernel(joined, scalars, ins, outs):
    z, sign = scalars[0][0], scalars[0][1]

    def put(shift, even, odd):
        for o in range(2):
            real, imag = interleave(even[o], odd[o])
            outs[o][0, around(z, shift)] = real
            outs[o][1, around(z, shift)] = imag

    if joined:
        v = ins[0]
        for shift in range(-3, 5):
            if shift in (0, 4):
                even, odd = (0, shift // 4), (1, shift // 4)
            elif shift < 0:
                even, odd = (0, -2 * shift), (0, -2 * shift + 1)
            else:
                even, odd = (1, 2 * shift + 1), (1, 2 * shift)
            put(shift, [v[:, *even, o] for o in range(2)], [v[:, *odd, o] for o in range(2)])
    else:
        own, far, *paid, got = ins
        put(0, *[[own[:, c, 0, o] for o in range(2)] for c in range(2)])
        put(4, *[[far[:, c, o] for o in range(2)] for c in range(2)])
        for d in STEPS:
            put(-sign * d, *[[paid[d - 1][0, :, c, o] for o in range(2)] for c in range(2)])
            put(sign * d, *[[got[d - 1, :, c, o] for o in range(2)] for c in range(2)])


def unpack(scalars, ins, chunk, old, after):
    joined = len(ins) == 1
    wide, one = (NXY, 2, NZ, 2, 8, 128), (NXY, 2, 2, 8, 128)
    if joined:
        ins = [ins[0].reshape(wide)]
        specs = [part(wide, 0)]
    else:
        own, far, *paid, got = ins
        ins = [own.reshape(wide), far.reshape(one)]
        ins += [x.reshape(2, *one) for x in paid]
        ins.append(got.reshape(3, *one))
        specs = [part(wide, 0, [(2, 1, 0)]), part(one, 0)]
        specs += [part((2, *one), 1, [(0, 1, 0)])] * 3 + [part((3, *one), 1)]
    return local_call(
        functools.partial(unpack_kernel, joined),
        scalars,
        ins,
        specs,
        list(old) + after,
        [GRID_IN] * 2,
        [chunk_part(chunk)] * 2,
        "unpack",
        {1 + len(ins) + i: i for i in range(len(old))},
    )


def to_ring(x, shift):
    moves = []
    for zh in range(2):
        for c in range(2):
            for zl in range(4):
                to = (zh * 4 + zl + (1 - 2 * c) * shift) % NZ
                moves.append((zh * 8 + c * 4 + zl, (to // 4) * 8 + c * 4 + to % 4))
    return lax.ppermute(x, ("zh", "c", "zl"), moves)


def to_far(x):
    return lax.ppermute(x, RING, [(i, (i + 4) % NZ) for i in range(NZ)])


def to_core(x):
    return lax.ppermute(x, "c", [(0, 1), (1, 0)])


def over_plane(x):
    return lax.all_to_all(x, PLANE, split_axis=0, concat_axis=0, tiled=True)


def shards(green_lesser, green_greater, screen, couple):
    z = lax.axis_index(RING).astype(jnp.int32)
    u = lax.axis_index(PLANE).astype(jnp.int32)
    scalars = jnp.stack([z, 1 - 2 * lax.rem(u, 2)])
    own, far, keep, give, gains = pack_ring(scalars, green_lesser, green_greater, screen, couple)
    far = to_far(far)
    got = to_core(give)
    rows = [
        jnp.concatenate([keep[d - 1].reshape(512, 128), got[d - 1].reshape(512, 128), gains[d]], axis=0)
        for d in STEPS
    ]
    second = over_plane(pack_plane(scalars, green_lesser, green_greater, rows))
    rows = [to_ring(x, d) for d, x in zip(STEPS, rows)]
    first = merge(own, far, rows)

    far2, paid2, first = fan(second, first)
    first = over_plane(first)
    far2 = to_far(far2)
    paid2 = [to_ring(x, d) for d, x in zip(STEPS, paid2)]
    gains = jnp.stack([gains[0, :4]] + [x[1024:1028] for x in rows])
    weights = lax.dynamic_slice(gains, (0, 0, u * KK), (4, 4, KK)).reshape(-1)
    give2 = give_back(paid2, far2)

    own, far, keep, give = convolve(scalars, weights, [first], False, 0, [give2])
    got = to_core(give)
    got2 = to_core(give2)
    paid = [jnp.concatenate([keep[d - 1], got[d - 1]], axis=0) for d in STEPS]
    order = list(paid)
    far = to_far(far)
    paid = [to_ring(x, d) for d, x in zip(STEPS, paid)]
    (second,) = convolve(scalars, weights, [second, far2, *paid2, got2], True, 1, order)
    second = over_plane(second)
    first = merge(own, far, paid)

    far2, paid2, first = fan(second, first)
    first = over_plane(first)
    far2 = to_far(far2)
    paid2 = [to_ring(x, d) for d, x in zip(STEPS, paid2)]
    give2 = give_back(paid2, far2)
    got2 = to_core(give2)
    done = unpack(scalars, [first], 0, [], [give2])
    polar, sigma = unpack(scalars, [second, far2, *paid2, got2], 1, done, [])
    return polar.reshape(2, 2048, 128), sigma.reshape(2, 2048, 128)


def solution(mesh):
    named = Mesh(mesh.devices.reshape(SIZES), AXES)
    placed = P(None, "zl", ("x", "zh", "y", "c"))
    return jax.shard_map(
        shards,
        mesh=named,
        in_specs=(placed, placed, P("zl"), P("zl")),
        out_specs=(placed, placed),
        check_vma=False,
    )
```

```python
import functools
import math

import jax
import jax.numpy as jnp
import ml_dtypes
import numpy as np
from jax import lax
from jax.experimental import pallas as pl
from jax.experimental.pallas import tpu as pltpu
from jax.sharding import Mesh
from jax.sharding import PartitionSpec as P

SIZES = (4, 2, 4, 2, 4)
AXES = ("x", "zh", "y", "c", "zl")
RING = ("zh", "zl")
PLANE = ("x", "y", "c")
NZ, NU = 8, 32
NXY = NU // 2
STEPS = (1, 2, 3)
PARTS = 1
BLOCK = (NU, 16, 128)
NJ, NB = 64, 128
NE = NJ * NB
KK = 4
F32, BF16 = jnp.float32, jnp.bfloat16
HBM = pl.BlockSpec(memory_space=pl.ANY)
VMEM = pl.BlockSpec(memory_space=pltpu.VMEM)
SMEM = pl.BlockSpec(memory_space=pltpu.SMEM)
LIMIT = 20 * 1024 * 1024
FULL = 58 * 1024 * 1024
LONG = 2 * 10**11


def halves(table):
    high = table.astype(np.float32).astype(ml_dtypes.bfloat16)
    low = (table - high.astype(np.float64)).astype(np.float32).astype(ml_dtypes.bfloat16)
    return high, low


@functools.lru_cache(maxsize=1)
def tables():
    zh, u = np.meshgrid(np.arange(2), np.arange(NU), indexing="ij")
    j = ((u // 8) * 16 + zh * 8 + u % 8).reshape(-1)
    outer = 2 * math.pi * (j[:, None] * np.arange(NJ)[None, :] % NJ) / NJ
    inner = 2 * math.pi * (np.arange(NB)[:, None] * np.arange(NB)[None, :] % NB) / NB
    twist = 2 * math.pi * (np.arange(NJ)[:, None] * np.arange(NB)[None, :]) / NE
    co, so, ci, si = np.cos(outer), np.sin(outer), np.cos(inner), np.sin(inner)
    d1 = np.block([[co.T, so.T], [-so.T, co.T]])
    d2 = np.block([[ci, -si], [si, ci]])
    e2 = np.block([[ci, si], [-si, ci]])
    polar_scale, sigma_scale = NE**-1.5, -(float(NE) ** -2)
    e1p = polar_scale * np.block([[-so, -co], [co, -so]])
    e1s = sigma_scale * np.block([[co, -so], [so, co]])
    products = [np.concatenate(halves(table), axis=1) for table in (d1, e1p, e1s)]
    for table in (d2, e2):
        products.extend(halves(table))
    turns = np.concatenate([np.cos(twist), np.sin(twist)], axis=1).astype(np.float32)
    return np.concatenate(products, axis=0), turns


def split(x):
    high = x.astype(BF16)
    return high, (x - high.astype(F32)).astype(BF16)


def dot(a, b):
    return lax.dot_general(a, b, (((1,), (0,)), ((), ())), preferred_element_type=F32)


def dot3(a, b):
    return dot(a[0], b[0]) + (dot(a[0], b[1]) + dot(a[1], b[0]))


def dot_pair(table, first, second):
    high, low = split(jnp.concatenate([first, second], axis=1))
    out = dot(table, jnp.concatenate([high, high], axis=0)) + dot(table[:, :128], low)
    return out[:, :NB], out[:, NB:]


def interleave(first, second):
    low = jnp.concatenate([first[:, :KK], second[:, :KK]], axis=1)
    high = jnp.concatenate([first[:, KK:], second[:, KK:]], axis=1)
    return low, high


def around(z, shift):
    return lax.rem(z + (shift + NZ), NZ)


def whole(shape):
    return pl.BlockSpec(shape, lambda i, *_: (0,) * len(shape))


def part(shape, dim, at=()):
    block, fixed = list(shape), [0] * len(shape)
    block[dim] //= PARTS
    for where, length, index in at:
        block[where], fixed[where] = length, index
    return pl.BlockSpec(
        tuple(block), lambda i, *_: tuple(i if n == dim else f for n, f in enumerate(fixed))
    )


def local_call(
    kernel, scalars, ins, in_specs, after, shapes, out_specs, name, aliases=None, work=0, limit=LIMIT
):
    count = len(ins)
    return pl.pallas_call(
        lambda *refs: kernel(refs[:1], refs[1 : 1 + count], refs[1 + count + len(after) :]),
        out_shape=[jax.ShapeDtypeStruct(s, F32) for s in shapes],
        grid_spec=pltpu.PrefetchScalarGridSpec(
            num_scalar_prefetch=1,
            grid=(PARTS,),
            in_specs=list(in_specs) + [HBM] * len(after),
            out_specs=out_specs,
        ),
        input_output_aliases=aliases or {},
        compiler_params=pltpu.CompilerParams(vmem_limit_bytes=limit),
        cost_estimate=pl.CostEstimate(flops=work, bytes_accessed=0, transcendentals=0),
        name=name,
    )(scalars, *ins, *after)


GRID_IN = (2, 2 * NZ, NXY, 8, 128)


def chunk_part(chunk):
    return part(GRID_IN, 2, [(1, NZ, chunk)])


def blocks_of(lesser, greater, zd):
    for g, ref in enumerate((lesser, greater)):
        yield g, *interleave(ref[0, zd], ref[1, zd])


def pack_ring_kernel(scalars, ins, outs):
    lesser, greater, screen, couple = ins
    own, far, keep, give, gains = outs
    z, sign = scalars[0][0], scalars[0][1]
    targets = [(own, 0), (far, 4)]
    targets += [(keep.at[d - 1], sign * d) for d in STEPS]
    targets += [(give.at[d - 1], -sign * d) for d in STEPS]
    for dest, shift in targets:
        for g, even, odd in blocks_of(lesser, greater, around(z, shift)):
            dest[:, 0, g] = even
            dest[:, 1, g] = odd
    for d in range(4):
        zd = around(z, sign * d)
        rows = [ref[pl.ds(zd + q * NZ, 1), :] for ref in (screen, couple) for q in range(2)]
        gains[d] = jnp.concatenate(rows * 4, axis=0)


def pack_ring(scalars, lesser, greater, screen, couple):
    small = whole((16, 128))
    one = (NXY, 2, 2, 8, 128)
    shapes = [one, one, (3, *one), (3, *one), (4, 16, 128)]
    own, far, keep, give, gains = local_call(
        pack_ring_kernel,
        scalars,
        [lesser.reshape(GRID_IN), greater.reshape(GRID_IN), screen.reshape(16, 128), couple.reshape(16, 128)],
        [chunk_part(0), chunk_part(0), small, small],
        [],
        shapes,
        [part(one, 0), part(one, 0), part((3, *one), 1), part((3, *one), 1), whole((4, 16, 128))],
        "pack_ring",
        limit=FULL,
    )
    return own.reshape(BLOCK), far.reshape(BLOCK), keep.reshape(3, *BLOCK), give.reshape(3, *BLOCK), gains


def pack_plane_kernel(scalars, ins, outs):
    lesser, greater = ins
    out = outs[0]
    z = scalars[0][0]
    for shift in range(-3, 5):
        for g, even, odd in blocks_of(lesser, greater, around(z, shift)):
            if shift in (0, 4):
                out[:, 0, shift // 4, g] = even
                out[:, 1, shift // 4, g] = odd
            elif shift > 0:
                out[:, 0, 2 * shift, g] = even
                out[:, 0, 2 * shift + 1, g] = odd
            else:
                out[:, 1, -2 * shift, g] = odd
                out[:, 1, -2 * shift + 1, g] = even


def pack_plane(scalars, lesser, greater, after):
    shape = (NXY, 2, NZ, 2, 8, 128)
    (out,) = local_call(
        pack_plane_kernel,
        scalars,
        [lesser.reshape(GRID_IN), greater.reshape(GRID_IN)],
        [chunk_part(1), chunk_part(1)],
        after,
        [shape],
        [part(shape, 0)],
        "pack_plane",
        limit=FULL,
    )
    return out.reshape(NU, NZ, 16, 128)


def shuttle(ins, shapes, routes, name, through=None, after=(), work=LONG):
    count, n_after = len(ins), len(after) + (through is not None)
    extra = [] if through is None else [through]

    def kernel(*refs):
        outs = refs[count + n_after :]
        held, in_sem, out_sem = refs[-3:]
        pulls = [
            pltpu.make_async_copy(refs[i].at[a], held.at[n], in_sem.at[n]) for n, (i, a, _, _) in enumerate(routes)
        ]
        pushes = [
            pltpu.make_async_copy(held.at[n], outs[o].at[b], out_sem.at[n]) for n, (_, _, o, b) in enumerate(routes)
        ]
        for copy in pulls:
            copy.start()
        for pull, push in zip(pulls, pushes):
            pull.wait()
            push.start()
        for copy in pushes:
            copy.wait()

    return pl.pallas_call(
        kernel,
        out_shape=[jax.ShapeDtypeStruct(s, F32) for s in shapes + [x.shape for x in extra]],
        in_specs=[HBM] * (count + n_after),
        out_specs=[HBM] * (len(shapes) + len(extra)),
        scratch_shapes=[
            pltpu.VMEM((len(routes), *BLOCK), F32),
            pltpu.SemaphoreType.DMA((len(routes),)),
            pltpu.SemaphoreType.DMA((len(routes),)),
        ],
        input_output_aliases={count: len(shapes)} if extra else {},
        compiler_params=pltpu.CompilerParams(vmem_limit_bytes=LIMIT),
        cost_estimate=pl.CostEstimate(flops=work, bytes_accessed=0, transcendentals=0),
        name=name,
    )(*ins, *extra, *after)


ALL = slice(None)


def merge(own, far, paid):
    ins = [own.reshape(NU, 16, 128), far] + [x.reshape(-1, 16, 128) for x in paid]
    routes = [(0, ALL, 0, (ALL, 0)), (1, ALL, 0, (ALL, 1))]
    for d in STEPS:
        for m in range(2):
            routes.append((1 + d, pl.ds(m * NU, NU), 0, (ALL, 2 * d + m)))
    return shuttle(ins, [(NU, NZ, 16, 128)], routes, "merge")[0]


def give_back(paid, far):
    routes = [(i, 1, 0, i) for i in range(len(paid))]
    return shuttle(paid, [(len(paid), *BLOCK)], routes, "give", after=[far])[0]


def fan(joined, through):
    routes = [(0, (ALL, 1), 0, ALL)]
    for d in STEPS:
        for m in range(2):
            routes.append((0, (ALL, 2 * d + m), d, m))
    out = shuttle([joined], [BLOCK] + [(2, *BLOCK)] * 3, routes, "fan", through=through, work=0)
    return out[0], list(out[1:4]), out[4]


def convolve_kernel(joined_in, joined_out, chunk, n_after, *refs):
    n_in = 1 if joined_in else 7
    n_out = 1 if joined_out else 4
    refs = list(refs)
    scalars, weights = refs[:2]
    ins = refs[2 : 2 + n_in]
    tabs = refs[2 + n_in : 4 + n_in]
    outs = refs[4 + n_in + n_after : 4 + n_in + n_after + n_out]
    xin, yout, sem, tab_sem = refs[4 + n_in + n_after + n_out :][:4]
    held = refs[8 + n_in + n_after + n_out :]
    z, sign = scalars[0], scalars[1]

    tab_copies = [pltpu.make_async_copy(t, h, tab_sem.at[i]) for i, (t, h) in enumerate(zip(tabs, held))]
    x_at = xin.at[: NZ * NU].reshape(NZ, NXY, 2, 16, 128)
    y_at = yout.at[: NZ * NU].reshape(NZ, NXY, 2, 16, 128)

    def joined_places(direction):
        for c in range(2):
            way = direction * (1 - 2 * c)
            yield c, 0, z, c
            yield c, 1, around(z, 4), c
            for d in STEPS:
                for m in range(2):
                    yield c, 2 * d + m, around(z, way * d), c ^ m

    pairs = []
    if joined_in:
        source = ins[0].reshape(NXY, 2, NZ, 16, 128)
        for c, slot, zs, core in joined_places(-1):
            pairs.append((source.at[:, c, slot], x_at.at[zs, :, core]))
    else:
        own, far = ins[:2]
        got = [ins[5].at[0], ins[5].at[1], ins[6]]
        pairs.append((own.at[:, 0], xin.at[pl.ds(z * NU, NU)]))
        pairs.append((far, xin.at[pl.ds(around(z, 4) * NU, NU)]))
        for d in STEPS:
            pairs.append((ins[1 + d].at[0], xin.at[pl.ds(around(z, -sign * d) * NU, NU)]))
            pairs.append((got[d - 1], xin.at[pl.ds(around(z, sign * d) * NU, NU)]))
    copies = [pltpu.make_async_copy(s, t, sem.at[i]) for i, (s, t) in enumerate(pairs)]
    for copy in copies + tab_copies:
        copy.start()
    for copy in copies + tab_copies:
        copy.wait()

    products, turns = held
    d1, e1p, e1s = [products[i * 128 : i * 128 + 128] for i in range(3)]
    d2, e2 = [
        (products[i * 512 + 384 : i * 512 + 640], products[i * 512 + 640 : i * 512 + 896]) for i in range(2)
    ]
    cos, sin = turns[:, :NB], turns[:, NB:]
    rows_in = xin.reshape((NZ * NU + 1) * 16, 128)
    rows_out = yout.reshape((NZ * NU + 1) * 16, 128)

    def step(kk, carry):
        turned = []
        for g in range(2):
            for r in (0, 2):
                sides = []
                for row in (r, r + 1):
                    parts = []
                    for c in range(2):
                        for zh in range(2):
                            base = (zh * 4 + row) * NU * 16 + g * 8 + c * KK + kk
                            parts.append(rows_in[pl.ds(base, NU, stride=16), :])
                    sides.append(jnp.concatenate(parts, axis=0))
                for y in dot_pair(d1, *sides):
                    yr, yi = y[:NJ], y[NJ:]
                    turned.append(jnp.concatenate([yr * cos + yi * sin, yi * cos - yr * sin], axis=1))
        spec = dot3(split(jnp.concatenate(turned, axis=0)), d2)
        lr, li = spec[:256, :NB], spec[:256, NB:]
        gr, gi = spec[256:, :NB], spec[256:, NB:]
        cr = lr * gr + li * gi
        ci = li * gr - lr * gi
        wr, wi = [], []
        for r in range(4):
            d = lax.rem((z + (NZ - r)) * sign + 4 * NZ, 4)
            own_gain = weights[d * 16 + chunk * KK + kk]
            side_gain = weights[d * 16 + 8 + chunk * KK + kk]
            for source, dest in ((cr, wr), (ci, wi)):
                rows = [source[q * NJ : (q + 1) * NJ] for q in (r - 1, r + 1) if 0 <= q < 4]
                beside = rows[0] if len(rows) == 1 else rows[0] + rows[1]
                dest.append(own_gain * source[r * NJ : (r + 1) * NJ] + side_gain * beside)
        wr, wi = jnp.concatenate(wr, axis=0), jnp.concatenate(wi, axis=0)
        vr = lr * wr - li * wi
        vi = lr * wi + li * wr
        both = jnp.concatenate(
            [jnp.concatenate([cr, ci], axis=1), jnp.concatenate([vr, vi], axis=1)], axis=0
        )
        back = dot3(split(both), e2)
        for o in range(2):
            for r in (0, 2):
                sides = []
                for row in (r, r + 1):
                    part = back[(o * 4 + row) * NJ : (o * 4 + row + 1) * NJ]
                    ar, ai = part[:, :NB], part[:, NB:]
                    sides.append(jnp.concatenate([ar * cos - ai * sin, ai * cos + ar * sin], axis=0))
                for row, done in zip((r, r + 1), dot_pair((e1p, e1s)[o], *sides)):
                    for c in range(2):
                        for zh in range(2):
                            base = (zh * 4 + row) * NU * 16 + o * 8 + c * KK + kk
                            at = (c * 2 + zh) * NU
                            rows_out[pl.ds(base, NU, stride=16), :] = done[at : at + NU]
        return carry

    lax.fori_loop(0, KK, step, 0, unroll=True)

    pairs = []
    if joined_out:
        dest = outs[0].reshape(NXY, 2, NZ, 16, 128)
        for c, slot, zd, core in joined_places(1):
            pairs.append((y_at.at[zd, :, core], dest.at[:, c, slot]))
    else:
        own, far, keep, give = outs
        pairs.append((yout.at[pl.ds(z * NU, NU)], own))
        pairs.append((yout.at[pl.ds(around(z, 4) * NU, NU)], far))
        for d in STEPS:
            pairs.append((yout.at[pl.ds(around(z, sign * d) * NU, NU)], keep.at[d - 1]))
            pairs.append((yout.at[pl.ds(around(z, -sign * d) * NU, NU)], give.at[d - 1]))
    copies = [pltpu.make_async_copy(s, t, sem.at[i]) for i, (s, t) in enumerate(pairs)]
    for copy in copies:
        copy.start()
    for copy in copies:
        copy.wait()


def convolve(scalars, weights, ins, joined_out, chunk, after):
    consts = [jnp.asarray(t) for t in tables()]
    if joined_out:
        shapes = [(NU, NZ, 16, 128)]
    else:
        shapes = [BLOCK, BLOCK, (3, *BLOCK), (3, *BLOCK)]
    return pl.pallas_call(
        functools.partial(convolve_kernel, len(ins) == 1, joined_out, chunk, len(after)),
        out_shape=[jax.ShapeDtypeStruct(s, F32) for s in shapes],
        in_specs=[SMEM, SMEM] + [HBM] * (len(ins) + len(consts) + len(after)),
        out_specs=[HBM] * len(shapes),
        scratch_shapes=[
            pltpu.VMEM((NZ * NU + 1, 16, 128), F32),
            pltpu.VMEM((NZ * NU + 1, 16, 128), F32),
            pltpu.SemaphoreType.DMA((2 * NZ,)),
            pltpu.SemaphoreType.DMA((2,)),
        ]
        + [pltpu.VMEM(t.shape, t.dtype) for t in consts],
        compiler_params=pltpu.CompilerParams(vmem_limit_bytes=LIMIT),
        cost_estimate=pl.CostEstimate(flops=LONG, bytes_accessed=0, transcendentals=0),
        name="convolve",
    )(scalars, weights, *ins, *consts, *after)


def unpack_kernel(joined, scalars, ins, outs):
    z, sign = scalars[0][0], scalars[0][1]

    def put(shift, even, odd):
        for o in range(2):
            real, imag = interleave(even[o], odd[o])
            outs[o][0, around(z, shift)] = real
            outs[o][1, around(z, shift)] = imag

    if joined:
        v = ins[0]
        for shift in range(-3, 5):
            if shift in (0, 4):
                even, odd = (0, shift // 4), (1, shift // 4)
            elif shift < 0:
                even, odd = (0, -2 * shift), (0, -2 * shift + 1)
            else:
                even, odd = (1, 2 * shift + 1), (1, 2 * shift)
            put(shift, [v[:, *even, o] for o in range(2)], [v[:, *odd, o] for o in range(2)])
    else:
        own, far, *paid, got = ins
        put(0, *[[own[:, c, 0, o] for o in range(2)] for c in range(2)])
        put(4, *[[far[:, c, o] for o in range(2)] for c in range(2)])
        for d in STEPS:
            put(-sign * d, *[[paid[d - 1][0, :, c, o] for o in range(2)] for c in range(2)])
            put(sign * d, *[[got[d - 1, :, c, o] for o in range(2)] for c in range(2)])


def unpack(scalars, ins, chunk, old, after):
    joined = len(ins) == 1
    wide, one = (NXY, 2, NZ, 2, 8, 128), (NXY, 2, 2, 8, 128)
    if joined:
        ins = [ins[0].reshape(wide)]
        specs = [part(wide, 0)]
    else:
        own, far, *paid, got = ins
        ins = [own.reshape(wide), far.reshape(one)]
        ins += [x.reshape(2, *one) for x in paid]
        ins.append(got.reshape(3, *one))
        specs = [part(wide, 0, [(2, 1, 0)]), part(one, 0)]
        specs += [part((2, *one), 1, [(0, 1, 0)])] * 3 + [part((3, *one), 1)]
    return local_call(
        functools.partial(unpack_kernel, joined),
        scalars,
        ins,
        specs,
        list(old) + after,
        [GRID_IN] * 2,
        [chunk_part(chunk)] * 2,
        "unpack",
        {1 + len(ins) + i: i for i in range(len(old))},
    )


def to_ring(x, shift):
    moves = []
    for zh in range(2):
        for c in range(2):
            for zl in range(4):
                to = (zh * 4 + zl + (1 - 2 * c) * shift) % NZ
                moves.append((zh * 8 + c * 4 + zl, (to // 4) * 8 + c * 4 + to % 4))
    return lax.ppermute(x, ("zh", "c", "zl"), moves)


def to_far(x):
    return lax.ppermute(x, RING, [(i, (i + 4) % NZ) for i in range(NZ)])


def to_core(x):
    return lax.ppermute(x, "c", [(0, 1), (1, 0)])


def over_plane(x):
    return lax.all_to_all(x, PLANE, split_axis=0, concat_axis=0, tiled=True)


def shards(green_lesser, green_greater, screen, couple):
    z = lax.axis_index(RING).astype(jnp.int32)
    u = lax.axis_index(PLANE).astype(jnp.int32)
    scalars = jnp.stack([z, 1 - 2 * lax.rem(u, 2)])
    own, far, keep, give, gains = pack_ring(scalars, green_lesser, green_greater, screen, couple)
    far = to_far(far)
    got = to_core(give)
    rows = [
        jnp.concatenate([keep[d - 1].reshape(512, 128), got[d - 1].reshape(512, 128), gains[d]], axis=0)
        for d in STEPS
    ]
    second = over_plane(pack_plane(scalars, green_lesser, green_greater, rows))
    rows = [to_ring(x, d) for d, x in zip(STEPS, rows)]
    first = merge(own, far, rows)

    far2, paid2, first = fan(second, first)
    first = over_plane(first)
    far2 = to_far(far2)
    paid2 = [to_ring(x, d) for d, x in zip(STEPS, paid2)]
    gains = jnp.stack([gains[0, :4]] + [x[1024:1028] for x in rows])
    weights = lax.dynamic_slice(gains, (0, 0, u * KK), (4, 4, KK)).reshape(-1)
    give2 = give_back(paid2[:2], far2)

    own, far, keep, give = convolve(scalars, weights, [first], False, 0, [give2])
    got = to_core(give)
    got2 = [to_core(give2), to_core(paid2[2][1])]
    paid = [jnp.concatenate([keep[d - 1], got[d - 1]], axis=0) for d in STEPS]
    order = list(paid)
    far = to_far(far)
    paid = [to_ring(x, d) for d, x in zip(STEPS, paid)]
    (second,) = convolve(scalars, weights, [second, far2, *paid2, *got2], True, 1, order)
    second = over_plane(second)
    first = merge(own, far, paid)

    far2, paid2, first = fan(second, first)
    first = over_plane(first)
    far2 = to_far(far2)
    paid2 = [to_ring(x, d) for d, x in zip(STEPS, paid2)]
    give2 = give_back(paid2, far2)
    got2 = to_core(give2)
    done = unpack(scalars, [first], 0, [], [give2])
    polar, sigma = unpack(scalars, [second, far2, *paid2, got2], 1, done, [])
    return polar.reshape(2, 2048, 128), sigma.reshape(2, 2048, 128)


def solution(mesh):
    named = Mesh(mesh.devices.reshape(SIZES), AXES)
    placed = P(None, "zl", ("x", "zh", "y", "c"))
    return jax.shard_map(
        shards,
        mesh=named,
        in_specs=(placed, placed, P("zl"), P("zl")),
        out_specs=(placed, placed),
        check_vma=False,
    )
```

```python
import functools
import math

import jax
import jax.numpy as jnp
import ml_dtypes
import numpy as np
from jax import lax
from jax.experimental import pallas as pl
from jax.experimental.pallas import tpu as pltpu
from jax.sharding import Mesh
from jax.sharding import PartitionSpec as P

SIZES = (4, 2, 4, 2, 4)
AXES = ("x", "zh", "y", "c", "zl")
RING = ("zh", "zl")
PLANE = ("x", "y", "c")
NZ, NU = 8, 32
NXY = NU // 2
STEPS = (1, 2, 3)
BLOCK = (NU, 16, 128)
NJ, NB = 64, 128
NE = NJ * NB
KK = 4
F32, BF16 = jnp.float32, jnp.bfloat16
HBM = pl.BlockSpec(memory_space=pl.ANY)
VMEM = pl.BlockSpec(memory_space=pltpu.VMEM)
SMEM = pl.BlockSpec(memory_space=pltpu.SMEM)
LIMIT = 20 * 1024 * 1024
FULL = 58 * 1024 * 1024
LONG = 2 * 10**11


def halves(table):
    high = table.astype(np.float32).astype(ml_dtypes.bfloat16)
    low = (table - high.astype(np.float64)).astype(np.float32).astype(ml_dtypes.bfloat16)
    return high, low


@functools.lru_cache(maxsize=1)
def tables():
    zh, u = np.meshgrid(np.arange(2), np.arange(NU), indexing="ij")
    j = ((u // 8) * 16 + zh * 8 + u % 8).reshape(-1)
    outer = 2 * math.pi * (j[:, None] * np.arange(NJ)[None, :] % NJ) / NJ
    half = np.arange(NB // 2)
    evens = 2 * math.pi * (half[:, None] * 2 * half[None, :] % NB) / NB
    odds = 2 * math.pi * (half[:, None] * (2 * half[None, :] + 1) % NB) / NB
    twist = 2 * math.pi * (np.arange(NJ)[:, None] * np.arange(NB)[None, :]) / NE
    co, so = np.cos(outer), np.sin(outer)
    d1 = np.block([[co.T, so.T], [-so.T, co.T]])
    ce, se, cd, sd = np.cos(evens), np.sin(evens), np.cos(odds), np.sin(odds)
    inners = [
        np.block([[ce, -se], [se, ce]]),
        np.block([[cd, -sd], [-sd, -cd]]),
        np.block([[ce.T, se.T], [-se.T, ce.T]]),
        np.block([[cd.T, sd.T], [-sd.T, cd.T]]),
    ]
    polar_scale, sigma_scale = NE**-1.5, -(float(NE) ** -2)
    e1p = polar_scale * np.block([[-so, -co], [co, -so]])
    e1s = sigma_scale * np.block([[co, -so], [so, co]])
    products = []
    for table in (d1, e1p, e1s):
        high, low = halves(table)
        products.append(np.block([[high, high], [low, np.zeros_like(low)]]))
    for table in inners:
        high, low = halves(table)
        products.append(np.block([[high, low], [high, np.zeros_like(low)]]))
    turns = np.concatenate([np.cos(twist), np.sin(twist)], axis=1).astype(np.float32)
    return np.concatenate(products, axis=0), turns


def split(x):
    high = x.astype(BF16)
    return high, (x - high.astype(F32)).astype(BF16)


def dot(a, b):
    return lax.dot_general(a, b, (((1,), (0,)), ((), ())), preferred_element_type=F32)


def dot_pair(table, first, second):
    high, low = split(jnp.concatenate([first, second], axis=1))
    out = dot(table, jnp.concatenate([high, low], axis=0))
    out = out[:128] + out[128:]
    return out[:, :NB], out[:, NB:]


def interleave(first, second):
    low = jnp.concatenate([first[:, :KK], second[:, :KK]], axis=1)
    high = jnp.concatenate([first[:, KK:], second[:, KK:]], axis=1)
    return low, high


def around(z, shift):
    return lax.rem(z + (shift + NZ), NZ)


def staged_call(kernel, scalars, ins, after, shapes, scratch, sems, name, aliases=None, limit=LIMIT):
    count = len(ins)

    def body(*refs):
        outs = refs[1 + count + len(after) :][: len(shapes)]
        kernel(refs[0], refs[1 : 1 + count], outs, refs[1 + count + len(after) + len(shapes) :])

    return pl.pallas_call(
        body,
        out_shape=[jax.ShapeDtypeStruct(s, F32) for s in shapes],
        in_specs=[SMEM] + [HBM] * (count + len(after)),
        out_specs=[HBM] * len(shapes),
        scratch_shapes=[pltpu.VMEM(s, F32) for s in scratch] + [pltpu.SemaphoreType.DMA((n,)) for n in sems],
        input_output_aliases=aliases or {},
        compiler_params=pltpu.CompilerParams(vmem_limit_bytes=limit),
        cost_estimate=pl.CostEstimate(flops=0, bytes_accessed=0, transcendentals=0),
        name=name,
    )(scalars, *ins, *after)


GRID_IN = (2, 2 * NZ, NXY, 8, 128)
SHIFTS = (-1, -2, -3, 1, 2, 3, 4, 0)


def pull_all(pairs, sem):
    copies = [pltpu.make_async_copy(s, t, sem.at[n]) for n, (s, t) in enumerate(pairs)]
    for copy in copies:
        copy.start()
    return copies


def pack_blocks(scalars, lesser, greater, held, built, in_sem, chunk, unit, done):
    z = scalars[0]
    places = [around(z, unit * shift) for shift in SHIFTS]
    pairs = [
        (ref.at[:, chunk * NZ + zd], held.at[n, g])
        for n, zd in enumerate(places)
        for g, ref in enumerate((lesser, greater))
    ]
    copies = pull_all(pairs, in_sem)
    for n in range(NZ):
        for g in range(2):
            copies[2 * n + g].wait()
            even, odd = interleave(held[n, g, 0], held[n, g, 1])
            built[n, :, 0, 8 * g : 8 * g + 8] = even
            built[n, :, 1, 8 * g : 8 * g + 8] = odd
        done(n, SHIFTS[n])


def pack_ring_kernel(scalars, ins, outs, scratch):
    lesser, greater, screen, couple = ins
    own, far, keep, give, own_gains, sent_gains = outs
    held, built, small, gains, in_sem, out_sem, small_sem = scratch
    z, sign = scalars[0], scalars[1]
    small_in = [pltpu.make_async_copy(r, small.at[i], small_sem.at[i]) for i, r in enumerate((screen, couple))]
    for copy in small_in:
        copy.start()
    pushes = []

    def push(n, shift):
        dest = own if shift == 0 else far if shift == 4 else keep.at[shift - 1] if shift > 0 else give.at[-shift - 1]
        pushes.append(pltpu.make_async_copy(built.at[n], dest, out_sem.at[n]))
        pushes[-1].start()

    pack_blocks(scalars, lesser, greater, held, built, in_sem, 0, sign, push)
    for copy in small_in:
        copy.wait()
    for d in range(4):
        zd = around(z, sign * d)
        rows = [small[i, pl.ds(zd + q * NZ, 1), :] for i in range(2) for q in range(2)]
        gains[d] = jnp.concatenate(rows * 4, axis=0)
    last = [
        pltpu.make_async_copy(gains.at[0], own_gains, small_sem.at[2]),
        pltpu.make_async_copy(gains.at[1:], sent_gains, small_sem.at[3]),
    ]
    for copy in last:
        copy.start()
    for copy in pushes + last:
        copy.wait()


PACKED = (NXY, 2, 16, 128)
PACK_SCRATCH = [(NZ, 2, 2, NXY, 8, 128), (NZ, *PACKED)]


def pack_ring(scalars, lesser, greater, screen, couple):
    shapes = [PACKED, PACKED, (3, *PACKED), (3, *PACKED), (16, 128), (3, 16, 128)]
    own, far, keep, give, own_gains, gains = staged_call(
        pack_ring_kernel,
        scalars,
        [lesser.reshape(GRID_IN), greater.reshape(GRID_IN), screen.reshape(16, 128), couple.reshape(16, 128)],
        [],
        shapes,
        PACK_SCRATCH + [(2, 16, 128), (4, 16, 128)],
        [2 * NZ, NZ, 4],
        "pack_ring",
        limit=FULL,
    )
    keep, give = keep.reshape(3, *BLOCK), give.reshape(3, *BLOCK)
    return own.reshape(BLOCK), far.reshape(BLOCK), keep, give, own_gains, gains


def pack_plane_kernel(scalars, ins, outs, scratch):
    lesser, greater = ins
    held, built, in_sem, out_sem = scratch
    pushes = []

    def push(n, shift):
        for c in range(2):
            core, slot = (c, shift // 4) if shift in (0, 4) else (0, 2 * shift + c)
            if shift < 0:
                core, slot = 1, -2 * shift + 1 - c
            pushes.append(pltpu.make_async_copy(built.at[n, :, c], outs[0].at[:, core, slot], out_sem.at[2 * n + c]))
            pushes[-1].start()

    pack_blocks(scalars, lesser, greater, held, built, in_sem, 1, 1, push)
    for copy in pushes:
        copy.wait()


def pack_plane(scalars, lesser, greater, after):
    (out,) = staged_call(
        pack_plane_kernel,
        scalars,
        [lesser.reshape(GRID_IN), greater.reshape(GRID_IN)],
        after,
        [(NXY, 2, NZ, 16, 128)],
        PACK_SCRATCH,
        [2 * NZ, 2 * NZ],
        "pack_plane",
        limit=FULL,
    )
    return out.reshape(NU, NZ, 16, 128)


def shuttle(ins, shapes, routes, name, through=None, after=(), work=LONG):
    count, n_after = len(ins), len(after) + (through is not None)
    extra = [] if through is None else [through]

    def kernel(*refs):
        outs = refs[count + n_after :]
        held, in_sem, out_sem = refs[-3:]
        pulls = [
            pltpu.make_async_copy(refs[i].at[a], held.at[n], in_sem.at[n]) for n, (i, a, _, _) in enumerate(routes)
        ]
        pushes = [
            pltpu.make_async_copy(held.at[n], outs[o].at[b], out_sem.at[n]) for n, (_, _, o, b) in enumerate(routes)
        ]
        for copy in pulls:
            copy.start()
        for pull, push in zip(pulls, pushes):
            pull.wait()
            push.start()
        for copy in pushes:
            copy.wait()

    return pl.pallas_call(
        kernel,
        out_shape=[jax.ShapeDtypeStruct(s, F32) for s in shapes + [x.shape for x in extra]],
        in_specs=[HBM] * (count + n_after),
        out_specs=[HBM] * (len(shapes) + len(extra)),
        scratch_shapes=[
            pltpu.VMEM((len(routes), *BLOCK), F32),
            pltpu.SemaphoreType.DMA((len(routes),)),
            pltpu.SemaphoreType.DMA((len(routes),)),
        ],
        input_output_aliases={count: len(shapes)} if extra else {},
        compiler_params=pltpu.CompilerParams(vmem_limit_bytes=LIMIT),
        cost_estimate=pl.CostEstimate(flops=work, bytes_accessed=0, transcendentals=0),
        name=name,
    )(*ins, *extra, *after)


ALL = slice(None)


def merge(own, far, paid):
    ins = [own.reshape(NU, 16, 128), far] + [x.reshape(-1, 16, 128) for x in paid]
    routes = [(0, ALL, 0, (ALL, 0)), (1, ALL, 0, (ALL, 1))]
    for d in STEPS:
        for m in range(2):
            routes.append((1 + d, pl.ds(m * NU, NU), 0, (ALL, 2 * d + m)))
    return shuttle(ins, [(NU, NZ, 16, 128)], routes, "merge")[0]


def give_back(paid, far):
    routes = [(i, 1, 0, i) for i in range(len(paid))]
    return shuttle(paid, [(len(paid), *BLOCK)], routes, "give", after=[far])[0]


def fan(joined, through):
    routes = [(0, (ALL, 1), 0, ALL)]
    for d in STEPS:
        for m in range(2):
            routes.append((0, (ALL, 2 * d + m), d, m))
    out = shuttle([joined], [BLOCK] + [(2, *BLOCK)] * 3, routes, "fan", through=through, work=0)
    return out[0], list(out[1:4]), out[4]


def convolve_kernel(joined_in, joined_out, chunk, n_after, *refs):
    n_in = 1 if joined_in else 8
    n_out = 1 if joined_out else 4
    refs = list(refs)
    scalars, weights = refs[:2]
    ins = refs[2 : 2 + n_in]
    tabs = refs[2 + n_in : 4 + n_in]
    outs = refs[4 + n_in + n_after : 4 + n_in + n_after + n_out]
    xin, yout, sem, tab_sem = refs[4 + n_in + n_after + n_out :][:4]
    held = refs[8 + n_in + n_after + n_out :]
    z, sign = scalars[0], scalars[1]

    tab_copies = [pltpu.make_async_copy(t, h, tab_sem.at[i]) for i, (t, h) in enumerate(zip(tabs, held))]
    x_at = xin.at[: NZ * NU].reshape(NZ, NXY, 2, 16, 128)
    y_at = yout.at[: NZ * NU].reshape(NZ, NXY, 2, 16, 128)

    def joined_places(direction):
        for c in range(2):
            way = direction * (1 - 2 * c)
            yield c, 0, z, c
            yield c, 1, around(z, 4), c
            for d in STEPS:
                for m in range(2):
                    yield c, 2 * d + m, around(z, way * d), c ^ m

    pairs = []
    if joined_in:
        source = ins[0].reshape(NXY, 2, NZ, 16, 128)
        for c, slot, zs, core in joined_places(-1):
            pairs.append((source.at[:, c, slot], x_at.at[zs, :, core]))
    else:
        own, far = ins[:2]
        got = [ins[5].at[0], ins[6], ins[7]]
        pairs.append((own.at[:, 0], xin.at[pl.ds(z * NU, NU)]))
        pairs.append((far, xin.at[pl.ds(around(z, 4) * NU, NU)]))
        for d in STEPS:
            pairs.append((ins[1 + d].at[0], xin.at[pl.ds(around(z, -sign * d) * NU, NU)]))
            pairs.append((got[d - 1], xin.at[pl.ds(around(z, sign * d) * NU, NU)]))
    copies = [pltpu.make_async_copy(s, t, sem.at[i]) for i, (s, t) in enumerate(pairs)]
    for copy in copies + tab_copies:
        copy.start()
    for copy in copies + tab_copies:
        copy.wait()

    products, turns = held
    d1, e1p, e1s = [products[i * 256 : i * 256 + 256] for i in range(3)]
    evens, odds, evens_back, odds_back = [products[768 + i * 256 : 1024 + i * 256] for i in range(4)]
    cos, sin = turns[:, :NB], turns[:, NB:]

    def swap(x):
        return pltpu.roll(x, NB // 2, 1)

    def pick(first, second):
        lane = lax.broadcasted_iota(jnp.int32, first.shape, 1)
        return jnp.where(lane < NB // 2, first, second)

    def dot_terms(x, table):
        out = dot(jnp.concatenate(split(x), axis=1), table)
        return out[:, :NB] + out[:, NB:]
    rows_in = xin.reshape((NZ * NU + 1) * 16, 128)
    rows_out = yout.reshape((NZ * NU + 1) * 16, 128)

    def step(kk, carry):
        sums, differences = [], []
        for g in range(2):
            for r in (0, 2):
                sides = []
                for row in (r, r + 1):
                    parts = []
                    for c in range(2):
                        for zh in range(2):
                            base = (zh * 4 + row) * NU * 16 + g * 8 + c * KK + kk
                            parts.append(rows_in[pl.ds(base, NU, stride=16), :])
                    sides.append(jnp.concatenate(parts, axis=0))
                for y in dot_pair(d1, *sides):
                    yr, yi = y[:NJ], y[NJ:]
                    tr, ti = yr * cos + yi * sin, yi * cos - yr * sin
                    sr, si = swap(tr), swap(ti)
                    sums.append(pick(tr + sr, ti + si))
                    differences.append(pick(tr - sr, ti - si))
        even = dot_terms(jnp.concatenate(sums, axis=0), evens)
        odd = dot_terms(jnp.concatenate(differences, axis=0), odds)
        real, imag = pick(even, swap(odd)), pick(swap(even), odd)
        lr, gr = real[:256], real[256:]
        li, gi = imag[:256], imag[256:]
        cr = lr * gr + li * gi
        ci = li * gr - lr * gi
        wr, wi = [], []
        for r in range(4):
            d = lax.rem((z + (NZ - r)) * sign + 4 * NZ, 4)
            own_gain = weights[d * 16 + chunk * KK + kk]
            side_gain = weights[d * 16 + 8 + chunk * KK + kk]
            for source, dest in ((cr, wr), (ci, wi)):
                rows = [source[q * NJ : (q + 1) * NJ] for q in (r - 1, r + 1) if 0 <= q < 4]
                beside = rows[0] if len(rows) == 1 else rows[0] + rows[1]
                dest.append(own_gain * source[r * NJ : (r + 1) * NJ] + side_gain * beside)
        wr, wi = jnp.concatenate(wr, axis=0), jnp.concatenate(wi, axis=0)
        vr = lr * wr - li * wi
        vi = lr * wi + li * wr
        real = jnp.concatenate([cr, vr], axis=0)
        imag = jnp.concatenate([ci, vi], axis=0)
        even = dot_terms(pick(real, swap(imag)), evens_back)
        odd = dot_terms(pick(swap(real), imag), odds_back)
        near, away = even + odd, even - odd
        back_real, back_imag = pick(near, swap(away)), pick(swap(near), away)
        for o in range(2):
            for r in (0, 2):
                sides = []
                for row in (r, r + 1):
                    at = (o * 4 + row) * NJ
                    ar, ai = back_real[at : at + NJ], back_imag[at : at + NJ]
                    sides.append(jnp.concatenate([ar * cos - ai * sin, ai * cos + ar * sin], axis=0))
                for row, done in zip((r, r + 1), dot_pair((e1p, e1s)[o], *sides)):
                    for c in range(2):
                        for zh in range(2):
                            base = (zh * 4 + row) * NU * 16 + o * 8 + c * KK + kk
                            at = (c * 2 + zh) * NU
                            rows_out[pl.ds(base, NU, stride=16), :] = done[at : at + NU]
        return carry

    lax.fori_loop(0, KK, step, 0, unroll=True)

    pairs = []
    if joined_out:
        dest = outs[0].reshape(NXY, 2, NZ, 16, 128)
        for c, slot, zd, core in joined_places(1):
            pairs.append((y_at.at[zd, :, core], dest.at[:, c, slot]))
    else:
        own, far, keep, give = outs
        pairs.append((yout.at[pl.ds(z * NU, NU)], own))
        pairs.append((yout.at[pl.ds(around(z, 4) * NU, NU)], far))
        for d in STEPS:
            pairs.append((yout.at[pl.ds(around(z, sign * d) * NU, NU)], keep.at[d - 1]))
            pairs.append((yout.at[pl.ds(around(z, -sign * d) * NU, NU)], give.at[d - 1]))
    copies = [pltpu.make_async_copy(s, t, sem.at[i]) for i, (s, t) in enumerate(pairs)]
    for copy in copies:
        copy.start()
    for copy in copies:
        copy.wait()


def convolve(scalars, weights, ins, joined_out, chunk, after):
    consts = [jnp.asarray(t) for t in tables()]
    if joined_out:
        shapes = [(NU, NZ, 16, 128)]
    else:
        shapes = [BLOCK, BLOCK, (3, *BLOCK), (3, *BLOCK)]
    return pl.pallas_call(
        functools.partial(convolve_kernel, len(ins) == 1, joined_out, chunk, len(after)),
        out_shape=[jax.ShapeDtypeStruct(s, F32) for s in shapes],
        in_specs=[SMEM, SMEM] + [HBM] * (len(ins) + len(consts) + len(after)),
        out_specs=[HBM] * len(shapes),
        scratch_shapes=[
            pltpu.VMEM((NZ * NU + 1, 16, 128), F32),
            pltpu.VMEM((NZ * NU + 1, 16, 128), F32),
            pltpu.SemaphoreType.DMA((2 * NZ,)),
            pltpu.SemaphoreType.DMA((2,)),
        ]
        + [pltpu.VMEM(t.shape, t.dtype) for t in consts],
        compiler_params=pltpu.CompilerParams(vmem_limit_bytes=LIMIT),
        cost_estimate=pl.CostEstimate(flops=LONG, bytes_accessed=0, transcendentals=0),
        name="convolve",
    )(scalars, weights, *ins, *consts, *after)


def unpack_kernel(joined, chunk, scalars, ins, outs, scratch):
    held, built, in_sem, out_sem = scratch
    z, sign = scalars[0], scalars[1]
    pairs, places = [], []
    if joined:
        for n, shift in enumerate(SHIFTS):
            places.append(around(z, shift))
            for c in range(2):
                core, slot = (c, shift // 4) if shift in (0, 4) else (0, -2 * shift + c)
                if 0 < shift < 4:
                    core, slot = 1, 2 * shift + 1 - c
                pairs.append((ins[0].at[:, core, slot], held.at[n, :, c]))
    else:
        own, far, *paid, got = ins
        sources = [(0, own.at[:, :, 0]), (4, far)]
        sources += [(-sign * d, paid[d - 1].at[0]) for d in STEPS]
        sources += [(sign * d, got.at[d - 1]) for d in STEPS]
        for n, (shift, source) in enumerate(sources):
            places.append(around(z, shift))
            pairs.append((source, held.at[n]))
    copies = pull_all(pairs, in_sem)
    per = len(pairs) // NZ
    pushes = []
    for n in range(NZ):
        for copy in copies[per * n : per * n + per]:
            copy.wait()
        for o in range(2):
            real, imag = interleave(held[n, :, 0, 8 * o : 8 * o + 8], held[n, :, 1, 8 * o : 8 * o + 8])
            built[n, o, 0] = real
            built[n, o, 1] = imag
            dest = outs[o].at[:, chunk * NZ + places[n]]
            pushes.append(pltpu.make_async_copy(built.at[n, o], dest, out_sem.at[2 * n + o]))
            pushes[-1].start()
    for copy in pushes:
        copy.wait()


def unpack(scalars, ins, chunk, old, after):
    joined = len(ins) == 1
    wide = (NXY, 2, NZ, 16, 128)
    if joined:
        ins = [ins[0].reshape(wide)]
    else:
        own, far, *paid, got = ins
        ins = [own.reshape(wide), far.reshape(PACKED)]
        ins += [x.reshape(2, *PACKED) for x in paid]
        ins.append(got.reshape(3, *PACKED))
    return staged_call(
        functools.partial(unpack_kernel, joined, chunk),
        scalars,
        ins,
        list(old) + after,
        [GRID_IN] * 2,
        [(NZ, *PACKED), (NZ, 2, 2, NXY, 8, 128)],
        [2 * NZ, 2 * NZ],
        "unpack",
        {1 + len(ins) + i: i for i in range(len(old))},
    )


def to_ring(x, shift):
    moves = []
    for zh in range(2):
        for c in range(2):
            for zl in range(4):
                to = (zh * 4 + zl + (1 - 2 * c) * shift) % NZ
                moves.append((zh * 8 + c * 4 + zl, (to // 4) * 8 + c * 4 + to % 4))
    return lax.ppermute(x, ("zh", "c", "zl"), moves)


def to_far(x):
    return lax.ppermute(x, RING, [(i, (i + 4) % NZ) for i in range(NZ)])


def to_core(x):
    return lax.ppermute(x, "c", [(0, 1), (1, 0)])


def over_plane(x):
    return lax.all_to_all(x, PLANE, split_axis=0, concat_axis=0, tiled=True)


def shards(green_lesser, green_greater, screen, couple):
    z = lax.axis_index(RING).astype(jnp.int32)
    u = lax.axis_index(PLANE).astype(jnp.int32)
    scalars = jnp.stack([z, 1 - 2 * lax.rem(u, 2)])
    own, far, keep, give, own_gains, gains = pack_ring(scalars, green_lesser, green_greater, screen, couple)
    far = to_far(far)
    got = to_core(give)
    rows = [
        jnp.concatenate([keep[d - 1].reshape(512, 128), got[d - 1].reshape(512, 128), gains[d - 1]], axis=0)
        for d in STEPS
    ]
    second = over_plane(pack_plane(scalars, green_lesser, green_greater, rows))
    rows = [to_ring(x, d) for d, x in zip(STEPS, rows)]
    first = merge(own, far, rows)

    far2, paid2, first = fan(second, first)
    first = over_plane(first)
    far2 = to_far(far2)
    paid2 = [to_ring(x, d) for d, x in zip(STEPS, paid2)]
    weights = [lax.dynamic_slice(own_gains, (0, u * KK), (4, KK))]
    weights += [lax.dynamic_slice(x, (x.shape[0] - 16, u * KK), (4, KK)) for x in rows]
    weights = jnp.stack(weights).reshape(-1)
    give2 = give_back(paid2[:1], far2)

    own, far, keep, give = convolve(scalars, weights, [first], False, 0, [give2])
    got = to_core(give)
    got2 = [to_core(x) for x in (give2, paid2[1][1], paid2[2][1])]
    paid = [jnp.concatenate([keep[d - 1], got[d - 1]], axis=0) for d in STEPS]
    order = list(paid)
    far = to_far(far)
    paid = [to_ring(x, d) for d, x in zip(STEPS, paid)]
    (second,) = convolve(scalars, weights, [second, far2, *paid2, *got2], True, 1, order)
    second = over_plane(second)
    first = merge(own, far, paid)

    far2, paid2, first = fan(second, first)
    first = over_plane(first)
    far2 = to_far(far2)
    paid2 = [to_ring(x, d) for d, x in zip(STEPS, paid2)]
    give2 = give_back(paid2, far2)
    got2 = to_core(give2)
    done = unpack(scalars, [first], 0, [], [give2])
    polar, sigma = unpack(scalars, [second, far2, *paid2, got2], 1, done, [])
    return polar.reshape(2, 2048, 128), sigma.reshape(2, 2048, 128)


def solution(mesh):
    named = Mesh(mesh.devices.reshape(SIZES), AXES)
    placed = P(None, "zl", ("x", "zh", "y", "c"))
    return jax.shard_map(
        shards,
        mesh=named,
        in_specs=(placed, placed, P("zl"), P("zl")),
        out_specs=(placed, placed),
        check_vma=False,
    )
```

```python
import functools
import math

import jax
import jax.numpy as jnp
import ml_dtypes
import numpy as np
from jax import lax
from jax.experimental import pallas as pl
from jax.experimental.pallas import tpu as pltpu
from jax.sharding import Mesh
from jax.sharding import PartitionSpec as P

SIZES = (4, 2, 4, 2, 4)
AXES = ("x", "zh", "y", "c", "zl")
RING = ("zh", "zl")
PLANE = ("x", "y", "c")
NZ, NU = 8, 32
NXY = NU // 2
STEPS = (1, 2, 3)
BLOCK = (NU, 16, 128)
NJ, NB = 64, 128
NE = NJ * NB
KK = 4
F32, BF16 = jnp.float32, jnp.bfloat16
HBM = pl.BlockSpec(memory_space=pl.ANY)
VMEM = pl.BlockSpec(memory_space=pltpu.VMEM)
SMEM = pl.BlockSpec(memory_space=pltpu.SMEM)
LIMIT = 20 * 1024 * 1024
FULL = 58 * 1024 * 1024
LONG = 2 * 10**11


def halves(table):
    high = table.astype(np.float32).astype(ml_dtypes.bfloat16)
    low = (table - high.astype(np.float64)).astype(np.float32).astype(ml_dtypes.bfloat16)
    return high, low


@functools.lru_cache(maxsize=1)
def tables():
    zh, u = np.meshgrid(np.arange(2), np.arange(NU), indexing="ij")
    j = ((u // 8) * 16 + zh * 8 + u % 8).reshape(-1)
    outer = 2 * math.pi * (j[:, None] * np.arange(NJ)[None, :] % NJ) / NJ
    half = np.arange(NB // 2)
    evens = 2 * math.pi * (half[:, None] * 2 * half[None, :] % NB) / NB
    odds = 2 * math.pi * (half[:, None] * (2 * half[None, :] + 1) % NB) / NB
    twist = 2 * math.pi * (np.arange(NJ)[:, None] * np.arange(NB)[None, :]) / NE
    co, so = np.cos(outer), np.sin(outer)
    d1 = np.block([[co.T, so.T], [-so.T, co.T]])
    ce, se, cd, sd = np.cos(evens), np.sin(evens), np.cos(odds), np.sin(odds)
    inners = [
        np.block([[ce, -se], [se, ce]]),
        np.block([[cd, -sd], [-sd, -cd]]),
        np.block([[ce.T, se.T], [-se.T, ce.T]]),
        np.block([[cd.T, sd.T], [-sd.T, cd.T]]),
    ]
    polar_scale, sigma_scale = NE**-1.5, -(float(NE) ** -2)
    e1p = polar_scale * np.block([[-so, -co], [co, -so]])
    e1s = sigma_scale * np.block([[co, -so], [so, co]])
    products = []
    for table in (d1, e1p, e1s):
        high, low = halves(table)
        products.append(np.block([[high, high], [low, np.zeros_like(low)]]))
    for table in inners:
        high, low = halves(table)
        products.append(np.block([[high, low], [high, np.zeros_like(low)]]))
    turns = np.concatenate([np.cos(twist), np.sin(twist)], axis=1).astype(np.float32)
    return np.concatenate(products, axis=0), turns


def split(x):
    high = x.astype(BF16)
    return high, (x - high.astype(F32)).astype(BF16)


def dot(a, b):
    return lax.dot_general(a, b, (((1,), (0,)), ((), ())), preferred_element_type=F32)


def dot_pair(table, first, second):
    high, low = split(jnp.concatenate([first, second], axis=1))
    out = dot(table, jnp.concatenate([high, low], axis=0))
    out = out[:128] + out[128:]
    return out[:, :NB], out[:, NB:]


def interleave(first, second):
    low = jnp.concatenate([first[:, :KK], second[:, :KK]], axis=1)
    high = jnp.concatenate([first[:, KK:], second[:, KK:]], axis=1)
    return low, high


def around(z, shift):
    return lax.rem(z + (shift + NZ), NZ)


def staged_call(kernel, scalars, ins, after, shapes, scratch, sems, name, aliases=None, limit=LIMIT):
    count = len(ins)

    def body(*refs):
        outs = refs[1 + count + len(after) :][: len(shapes)]
        kernel(refs[0], refs[1 : 1 + count], outs, refs[1 + count + len(after) + len(shapes) :])

    return pl.pallas_call(
        body,
        out_shape=[jax.ShapeDtypeStruct(s, F32) for s in shapes],
        in_specs=[SMEM] + [HBM] * (count + len(after)),
        out_specs=[HBM] * len(shapes),
        scratch_shapes=[pltpu.VMEM(s, F32) for s in scratch] + [pltpu.SemaphoreType.DMA((n,)) for n in sems],
        input_output_aliases=aliases or {},
        compiler_params=pltpu.CompilerParams(vmem_limit_bytes=limit),
        cost_estimate=pl.CostEstimate(flops=0, bytes_accessed=0, transcendentals=0),
        name=name,
    )(scalars, *ins, *after)


GRID_IN = (2, 2 * NZ, NXY, 8, 128)
SHIFTS = (-1, -2, -3, 1, 2, 3, 4, 0)


def pull_all(pairs, sem):
    copies = [pltpu.make_async_copy(s, t, sem.at[n]) for n, (s, t) in enumerate(pairs)]
    for copy in copies:
        copy.start()
    return copies


def pack_blocks(scalars, lesser, greater, held, built, in_sem, chunk, unit, done, shifts=SHIFTS):
    z = scalars[0]
    places = [around(z, unit * shift) for shift in shifts]
    pairs = [
        (ref.at[:, chunk * NZ + zd], held.at[n, g])
        for n, zd in enumerate(places)
        for g, ref in enumerate((lesser, greater))
    ]
    copies = pull_all(pairs, in_sem)
    for n in range(len(shifts)):
        for g in range(2):
            copies[2 * n + g].wait()
            even, odd = interleave(held[n, g, 0], held[n, g, 1])
            built[n, :, 0, 8 * g : 8 * g + 8] = even
            built[n, :, 1, 8 * g : 8 * g + 8] = odd
        done(n, shifts[n])


PACKED = (NXY, 2, 16, 128)
PACK_SCRATCH = [(NZ, 2, 2, NXY, 8, 128), (NZ, *PACKED)]


def pack_give_kernel(scalars, ins, outs, scratch):
    held, built, in_sem, out_sem = scratch
    pushes = []

    def push(n, shift):
        pushes.append(pltpu.make_async_copy(built.at[n], outs[0].at[-shift - 1], out_sem.at[n]))
        pushes[-1].start()

    pack_blocks(scalars, *ins, held, built, in_sem, 0, scalars[1], push, SHIFTS[:3])
    for copy in pushes:
        copy.wait()


def pack_give(scalars, lesser, greater):
    (give,) = staged_call(
        pack_give_kernel,
        scalars,
        [lesser.reshape(GRID_IN), greater.reshape(GRID_IN)],
        [],
        [(3, *PACKED)],
        PACK_SCRATCH,
        [2 * NZ, NZ],
        "pack_give",
        limit=FULL,
    )
    return give


def pack_ring_kernel(scalars, ins, outs, scratch):
    lesser, greater, screen, couple = ins
    own, far, keep, own_gains, sent_gains = outs
    held, built, small, gains, in_sem, out_sem, small_sem = scratch
    z, sign = scalars[0], scalars[1]
    small_in = [pltpu.make_async_copy(r, small.at[i], small_sem.at[i]) for i, r in enumerate((screen, couple))]
    for copy in small_in:
        copy.start()
    pushes = []

    def push(n, shift):
        dest = own if shift == 0 else far if shift == 4 else keep.at[shift - 1]
        pushes.append(pltpu.make_async_copy(built.at[n], dest, out_sem.at[n]))
        pushes[-1].start()

    pack_blocks(scalars, lesser, greater, held, built, in_sem, 0, sign, push, SHIFTS[3:])
    for copy in small_in:
        copy.wait()
    for d in range(4):
        zd = around(z, sign * d)
        rows = [small[i, pl.ds(zd + q * NZ, 1), :] for i in range(2) for q in range(2)]
        gains[d] = jnp.concatenate(rows * 4, axis=0)
    last = [
        pltpu.make_async_copy(gains.at[0], own_gains, small_sem.at[2]),
        pltpu.make_async_copy(gains.at[1:], sent_gains, small_sem.at[3]),
    ]
    for copy in last:
        copy.start()
    for copy in pushes + last:
        copy.wait()


def pack_ring(scalars, lesser, greater, screen, couple):
    give = pack_give(scalars, lesser, greater)
    shapes = [PACKED, PACKED, (3, *PACKED), (16, 128), (3, 16, 128)]
    own, far, keep, own_gains, gains = staged_call(
        pack_ring_kernel,
        scalars,
        [lesser.reshape(GRID_IN), greater.reshape(GRID_IN), screen.reshape(16, 128), couple.reshape(16, 128)],
        [give],
        shapes,
        PACK_SCRATCH + [(2, 16, 128), (4, 16, 128)],
        [2 * NZ, NZ, 4],
        "pack_ring",
        limit=FULL,
    )
    keep, give = keep.reshape(3, *BLOCK), give.reshape(3, *BLOCK)
    return own.reshape(BLOCK), far.reshape(BLOCK), keep, give, own_gains, gains


def pack_plane_kernel(scalars, ins, outs, scratch):
    lesser, greater = ins
    held, built, in_sem, out_sem = scratch
    pushes = []

    def push(n, shift):
        for c in range(2):
            core, slot = (c, shift // 4) if shift in (0, 4) else (0, 2 * shift + c)
            if shift < 0:
                core, slot = 1, -2 * shift + 1 - c
            pushes.append(pltpu.make_async_copy(built.at[n, :, c], outs[0].at[:, core, slot], out_sem.at[2 * n + c]))
            pushes[-1].start()

    pack_blocks(scalars, lesser, greater, held, built, in_sem, 1, 1, push)
    for copy in pushes:
        copy.wait()


def pack_plane(scalars, lesser, greater, after):
    (out,) = staged_call(
        pack_plane_kernel,
        scalars,
        [lesser.reshape(GRID_IN), greater.reshape(GRID_IN)],
        after,
        [(NXY, 2, NZ, 16, 128)],
        PACK_SCRATCH,
        [2 * NZ, 2 * NZ],
        "pack_plane",
        limit=FULL,
    )
    return out.reshape(NU, NZ, 16, 128)


def shuttle(ins, shapes, routes, name, through=None, after=(), work=LONG):
    count, n_after = len(ins), len(after) + (through is not None)
    extra = [] if through is None else [through]

    def kernel(*refs):
        outs = refs[count + n_after :]
        held, in_sem, out_sem = refs[-3:]
        pulls = [
            pltpu.make_async_copy(refs[i].at[a], held.at[n], in_sem.at[n]) for n, (i, a, _, _) in enumerate(routes)
        ]
        pushes = [
            pltpu.make_async_copy(held.at[n], outs[o].at[b], out_sem.at[n]) for n, (_, _, o, b) in enumerate(routes)
        ]
        for copy in pulls:
            copy.start()
        for pull, push in zip(pulls, pushes):
            pull.wait()
            push.start()
        for copy in pushes:
            copy.wait()

    return pl.pallas_call(
        kernel,
        out_shape=[jax.ShapeDtypeStruct(s, F32) for s in shapes + [x.shape for x in extra]],
        in_specs=[HBM] * (count + n_after),
        out_specs=[HBM] * (len(shapes) + len(extra)),
        scratch_shapes=[
            pltpu.VMEM((len(routes), *BLOCK), F32),
            pltpu.SemaphoreType.DMA((len(routes),)),
            pltpu.SemaphoreType.DMA((len(routes),)),
        ],
        input_output_aliases={count: len(shapes)} if extra else {},
        compiler_params=pltpu.CompilerParams(vmem_limit_bytes=LIMIT),
        cost_estimate=pl.CostEstimate(flops=work, bytes_accessed=0, transcendentals=0),
        name=name,
    )(*ins, *extra, *after)


ALL = slice(None)


def merge(own, far, paid):
    ins = [own.reshape(NU, 16, 128), far] + [x.reshape(-1, 16, 128) for x in paid]
    routes = [(0, ALL, 0, (ALL, 0)), (1, ALL, 0, (ALL, 1))]
    for d in STEPS:
        for m in range(2):
            routes.append((1 + d, pl.ds(m * NU, NU), 0, (ALL, 2 * d + m)))
    return shuttle(ins, [(NU, NZ, 16, 128)], routes, "merge")[0]


def give_back(paid, far):
    routes = [(i, 1, 0, i) for i in range(len(paid))]
    return shuttle(paid, [(len(paid), *BLOCK)], routes, "give", after=[far])[0]


def fan(joined, through):
    routes = [(0, (ALL, 1), 0, ALL)]
    for d in STEPS:
        for m in range(2):
            routes.append((0, (ALL, 2 * d + m), d, m))
    out = shuttle([joined], [BLOCK] + [(2, *BLOCK)] * 3, routes, "fan", through=through, work=0)
    return out[0], list(out[1:4]), out[4]


def convolve_kernel(joined_in, joined_out, chunk, n_after, *refs):
    n_in = 1 if joined_in else 8
    n_out = 1 if joined_out else 4
    refs = list(refs)
    scalars, weights = refs[:2]
    ins = refs[2 : 2 + n_in]
    tabs = refs[2 + n_in : 4 + n_in]
    outs = refs[4 + n_in + n_after : 4 + n_in + n_after + n_out]
    xin, yout, sem, tab_sem = refs[4 + n_in + n_after + n_out :][:4]
    held = refs[8 + n_in + n_after + n_out :]
    z, sign = scalars[0], scalars[1]

    tab_copies = [pltpu.make_async_copy(t, h, tab_sem.at[i]) for i, (t, h) in enumerate(zip(tabs, held))]
    x_at = xin.at[: NZ * NU].reshape(NZ, NXY, 2, 16, 128)
    y_at = yout.at[: NZ * NU].reshape(NZ, NXY, 2, 16, 128)

    def joined_places(direction):
        for c in range(2):
            way = direction * (1 - 2 * c)
            yield c, 0, z, c
            yield c, 1, around(z, 4), c
            for d in STEPS:
                for m in range(2):
                    yield c, 2 * d + m, around(z, way * d), c ^ m

    pairs = []
    if joined_in:
        source = ins[0].reshape(NXY, 2, NZ, 16, 128)
        for c, slot, zs, core in joined_places(-1):
            pairs.append((source.at[:, c, slot], x_at.at[zs, :, core]))
    else:
        own, far = ins[:2]
        got = [ins[5].at[0], ins[6], ins[7]]
        pairs.append((own.at[:, 0], xin.at[pl.ds(z * NU, NU)]))
        pairs.append((far, xin.at[pl.ds(around(z, 4) * NU, NU)]))
        for d in STEPS:
            pairs.append((ins[1 + d].at[0], xin.at[pl.ds(around(z, -sign * d) * NU, NU)]))
            pairs.append((got[d - 1], xin.at[pl.ds(around(z, sign * d) * NU, NU)]))
    copies = [pltpu.make_async_copy(s, t, sem.at[i]) for i, (s, t) in enumerate(pairs)]
    for copy in copies + tab_copies:
        copy.start()
    for copy in copies + tab_copies:
        copy.wait()

    products, turns = held
    d1, e1p, e1s = [products[i * 256 : i * 256 + 256] for i in range(3)]
    evens, odds, evens_back, odds_back = [products[768 + i * 256 : 1024 + i * 256] for i in range(4)]
    cos, sin = turns[:, :NB], turns[:, NB:]

    def swap(x):
        return pltpu.roll(x, NB // 2, 1)

    def pick(first, second):
        lane = lax.broadcasted_iota(jnp.int32, first.shape, 1)
        return jnp.where(lane < NB // 2, first, second)

    def dot_terms(x, table):
        out = dot(jnp.concatenate(split(x), axis=1), table)
        return out[:, :NB] + out[:, NB:]
    rows_in = xin.reshape((NZ * NU + 1) * 16, 128)
    rows_out = yout.reshape((NZ * NU + 1) * 16, 128)

    def step(kk, carry):
        sums, differences = [], []
        for g in range(2):
            for r in (0, 2):
                sides = []
                for row in (r, r + 1):
                    parts = []
                    for c in range(2):
                        for zh in range(2):
                            base = (zh * 4 + row) * NU * 16 + g * 8 + c * KK + kk
                            parts.append(rows_in[pl.ds(base, NU, stride=16), :])
                    sides.append(jnp.concatenate(parts, axis=0))
                for y in dot_pair(d1, *sides):
                    yr, yi = y[:NJ], y[NJ:]
                    tr, ti = yr * cos + yi * sin, yi * cos - yr * sin
                    sr, si = swap(tr), swap(ti)
                    sums.append(pick(tr + sr, ti + si))
                    differences.append(pick(tr - sr, ti - si))
        even = dot_terms(jnp.concatenate(sums, axis=0), evens)
        odd = dot_terms(jnp.concatenate(differences, axis=0), odds)
        real, imag = pick(even, swap(odd)), pick(swap(even), odd)
        lr, gr = real[:256], real[256:]
        li, gi = imag[:256], imag[256:]
        cr = lr * gr + li * gi
        ci = li * gr - lr * gi
        wr, wi = [], []
        for r in range(4):
            d = lax.rem((z + (NZ - r)) * sign + 4 * NZ, 4)
            own_gain = weights[d * 16 + chunk * KK + kk]
            side_gain = weights[d * 16 + 8 + chunk * KK + kk]
            for source, dest in ((cr, wr), (ci, wi)):
                rows = [source[q * NJ : (q + 1) * NJ] for q in (r - 1, r + 1) if 0 <= q < 4]
                beside = rows[0] if len(rows) == 1 else rows[0] + rows[1]
                dest.append(own_gain * source[r * NJ : (r + 1) * NJ] + side_gain * beside)
        wr, wi = jnp.concatenate(wr, axis=0), jnp.concatenate(wi, axis=0)
        vr = lr * wr - li * wi
        vi = lr * wi + li * wr
        real = jnp.concatenate([cr, vr], axis=0)
        imag = jnp.concatenate([ci, vi], axis=0)
        even = dot_terms(pick(real, swap(imag)), evens_back)
        odd = dot_terms(pick(swap(real), imag), odds_back)
        near, away = even + odd, even - odd
        back_real, back_imag = pick(near, swap(away)), pick(swap(near), away)
        for o in range(2):
            for r in (0, 2):
                sides = []
                for row in (r, r + 1):
                    at = (o * 4 + row) * NJ
                    ar, ai = back_real[at : at + NJ], back_imag[at : at + NJ]
                    sides.append(jnp.concatenate([ar * cos - ai * sin, ai * cos + ar * sin], axis=0))
                for row, done in zip((r, r + 1), dot_pair((e1p, e1s)[o], *sides)):
                    for c in range(2):
                        for zh in range(2):
                            base = (zh * 4 + row) * NU * 16 + o * 8 + c * KK + kk
                            at = (c * 2 + zh) * NU
                            rows_out[pl.ds(base, NU, stride=16), :] = done[at : at + NU]
        return carry

    lax.fori_loop(0, KK, step, 0, unroll=True)

    pairs = []
    if joined_out:
        dest = outs[0].reshape(NXY, 2, NZ, 16, 128)
        for c, slot, zd, core in joined_places(1):
            pairs.append((y_at.at[zd, :, core], dest.at[:, c, slot]))
    else:
        own, far, keep, give = outs
        pairs.append((yout.at[pl.ds(z * NU, NU)], own))
        pairs.append((yout.at[pl.ds(around(z, 4) * NU, NU)], far))
        for d in STEPS:
            pairs.append((yout.at[pl.ds(around(z, sign * d) * NU, NU)], keep.at[d - 1]))
            pairs.append((yout.at[pl.ds(around(z, -sign * d) * NU, NU)], give.at[d - 1]))
    copies = [pltpu.make_async_copy(s, t, sem.at[i]) for i, (s, t) in enumerate(pairs)]
    for copy in copies:
        copy.start()
    for copy in copies:
        copy.wait()


def convolve(scalars, weights, ins, joined_out, chunk, after):
    consts = [jnp.asarray(t) for t in tables()]
    if joined_out:
        shapes = [(NU, NZ, 16, 128)]
    else:
        shapes = [BLOCK, BLOCK, (3, *BLOCK), (3, *BLOCK)]
    return pl.pallas_call(
        functools.partial(convolve_kernel, len(ins) == 1, joined_out, chunk, len(after)),
        out_shape=[jax.ShapeDtypeStruct(s, F32) for s in shapes],
        in_specs=[SMEM, SMEM] + [HBM] * (len(ins) + len(consts) + len(after)),
        out_specs=[HBM] * len(shapes),
        scratch_shapes=[
            pltpu.VMEM((NZ * NU + 1, 16, 128), F32),
            pltpu.VMEM((NZ * NU + 1, 16, 128), F32),
            pltpu.SemaphoreType.DMA((2 * NZ,)),
            pltpu.SemaphoreType.DMA((2,)),
        ]
        + [pltpu.VMEM(t.shape, t.dtype) for t in consts],
        compiler_params=pltpu.CompilerParams(vmem_limit_bytes=LIMIT),
        cost_estimate=pl.CostEstimate(flops=LONG, bytes_accessed=0, transcendentals=0),
        name="convolve",
    )(scalars, weights, *ins, *consts, *after)


def unpack_kernel(joined, chunk, scalars, ins, outs, scratch):
    held, built, in_sem, out_sem = scratch
    z, sign = scalars[0], scalars[1]
    pairs, places = [], []
    if joined:
        for n, shift in enumerate(SHIFTS):
            places.append(around(z, shift))
            for c in range(2):
                core, slot = (c, shift // 4) if shift in (0, 4) else (0, -2 * shift + c)
                if 0 < shift < 4:
                    core, slot = 1, 2 * shift + 1 - c
                pairs.append((ins[0].at[:, core, slot], held.at[n, :, c]))
    else:
        own, far, *paid, got = ins
        sources = [(0, own.at[:, :, 0]), (4, far)]
        sources += [(-sign * d, paid[d - 1].at[0]) for d in STEPS]
        sources += [(sign * d, got.at[d - 1]) for d in STEPS]
        for n, (shift, source) in enumerate(sources):
            places.append(around(z, shift))
            pairs.append((source, held.at[n]))
    copies = pull_all(pairs, in_sem)
    per = len(pairs) // NZ
    pushes = []
    for n in range(NZ):
        for copy in copies[per * n : per * n + per]:
            copy.wait()
        for o in range(2):
            real, imag = interleave(held[n, :, 0, 8 * o : 8 * o + 8], held[n, :, 1, 8 * o : 8 * o + 8])
            built[n, o, 0] = real
            built[n, o, 1] = imag
            dest = outs[o].at[:, chunk * NZ + places[n]]
            pushes.append(pltpu.make_async_copy(built.at[n, o], dest, out_sem.at[2 * n + o]))
            pushes[-1].start()
    for copy in pushes:
        copy.wait()


def unpack(scalars, ins, chunk, old, after):
    joined = len(ins) == 1
    wide = (NXY, 2, NZ, 16, 128)
    if joined:
        ins = [ins[0].reshape(wide)]
    else:
        own, far, *paid, got = ins
        ins = [own.reshape(wide), far.reshape(PACKED)]
        ins += [x.reshape(2, *PACKED) for x in paid]
        ins.append(got.reshape(3, *PACKED))
    return staged_call(
        functools.partial(unpack_kernel, joined, chunk),
        scalars,
        ins,
        list(old) + after,
        [GRID_IN] * 2,
        [(NZ, *PACKED), (NZ, 2, 2, NXY, 8, 128)],
        [2 * NZ, 2 * NZ],
        "unpack",
        {1 + len(ins) + i: i for i in range(len(old))},
    )


def to_ring(x, shift):
    moves = []
    for zh in range(2):
        for c in range(2):
            for zl in range(4):
                to = (zh * 4 + zl + (1 - 2 * c) * shift) % NZ
                moves.append((zh * 8 + c * 4 + zl, (to // 4) * 8 + c * 4 + to % 4))
    return lax.ppermute(x, ("zh", "c", "zl"), moves)


def to_far(x):
    return lax.ppermute(x, RING, [(i, (i + 4) % NZ) for i in range(NZ)])


def to_core(x):
    return lax.ppermute(x, "c", [(0, 1), (1, 0)])


def over_plane(x):
    return lax.all_to_all(x, PLANE, split_axis=0, concat_axis=0, tiled=True)


def shards(green_lesser, green_greater, screen, couple):
    z = lax.axis_index(RING).astype(jnp.int32)
    u = lax.axis_index(PLANE).astype(jnp.int32)
    scalars = jnp.stack([z, 1 - 2 * lax.rem(u, 2)])
    own, far, keep, give, own_gains, gains = pack_ring(scalars, green_lesser, green_greater, screen, couple)
    far = to_far(far)
    got = to_core(give)
    rows = [
        jnp.concatenate([keep[d - 1].reshape(512, 128), got[d - 1].reshape(512, 128), gains[d - 1]], axis=0)
        for d in STEPS
    ]
    second = over_plane(pack_plane(scalars, green_lesser, green_greater, rows))
    rows = [to_ring(x, d) for d, x in zip(STEPS, rows)]
    first = merge(own, far, rows)

    far2, paid2, first = fan(second, first)
    first = over_plane(first)
    far2 = to_far(far2)
    paid2 = [to_ring(x, d) for d, x in zip(STEPS, paid2)]
    weights = [lax.dynamic_slice(own_gains, (0, u * KK), (4, KK))]
    weights += [lax.dynamic_slice(x, (x.shape[0] - 16, u * KK), (4, KK)) for x in rows]
    weights = jnp.stack(weights).reshape(-1)
    give2 = give_back(paid2[:1], far2)

    own, far, keep, give = convolve(scalars, weights, [first], False, 0, [give2])
    got = to_core(give)
    got2 = [to_core(x) for x in (give2, paid2[1][1], paid2[2][1])]
    paid = [jnp.concatenate([keep[d - 1], got[d - 1]], axis=0) for d in STEPS]
    order = list(paid)
    far = to_far(far)
    paid = [to_ring(x, d) for d, x in zip(STEPS, paid)]
    (second,) = convolve(scalars, weights, [second, far2, *paid2, *got2], True, 1, order)
    second = over_plane(second)
    first = merge(own, far, paid)

    far2, paid2, first = fan(second, first)
    first = over_plane(first)
    far2 = to_far(far2)
    paid2 = [to_ring(x, d) for d, x in zip(STEPS, paid2)]
    give2 = give_back(paid2, far2)
    got2 = to_core(give2)
    done = unpack(scalars, [first], 0, [], [give2])
    polar, sigma = unpack(scalars, [second, far2, *paid2, got2], 1, done, [])
    return polar.reshape(2, 2048, 128), sigma.reshape(2, 2048, 128)


def solution(mesh):
    named = Mesh(mesh.devices.reshape(SIZES), AXES)
    placed = P(None, "zl", ("x", "zh", "y", "c"))
    return jax.shard_map(
        shards,
        mesh=named,
        in_specs=(placed, placed, P("zl"), P("zl")),
        out_specs=(placed, placed),
        check_vma=False,
    )
```
